32 devices in a mesh: grp: 2 (over y), seq: 4 (over z), head: 2 (over x), dat: 2 (over core).
Axes of the slice: x: 2, y: 2, z: 4, core: 2. Of those that a mesh axis runs over, the one named last changes fastest.
Arguments:
- queries: bfloat16 [4, 256, 3072], P(('grp', 'dat'), 'seq', 'head'), parts along dimension 0, may hold values from -10 to 10
- keys: bfloat16 [4, 256, 512], P(('grp', 'dat'), 'seq', 'head'), parts along dimension 0, may hold values from -6 to 6
- values: bfloat16 [4, 256, 512], P(('grp', 'dat'), 'seq', 'head'), parts along dimension 0, may hold values from -6 to 6
- residual_in: bfloat16 [4, 256, 3072], P(('grp', 'dat'), 'seq', 'head'), parts along dimension 0, may hold values from -40 to 40
- out_proj: bfloat16 [24, 128, 3072], P('head', 'seq'), may hold values from -0.5 to 0.5
- norm_gain: bfloat16 [3072], replicated, may hold values from 0.5 to 1.5
- expert_gate: bfloat16 [4, 3072, 8192], P('head', None, 'seq'), may hold values from -0.109375 to 0.109375
- expert_up: bfloat16 [4, 3072, 8192], P('head', None, 'seq'), may hold values from -0.109375 to 0.109375
- routes: int32 [4, 256, 2], P(('grp', 'dat'), 'seq'), parts along dimension 0, may hold values from 0 to 3, as said below
- gate_numer: int32 [4, 256], P(('grp', 'dat'), 'seq'), parts along dimension 0, may hold values from 64 to 191
- sequence_lengths: int32 [4], P(('grp', 'dat')), parts along dimension 0, may hold values from 128 to 256, as said below
Outputs:
- stream: bfloat16 [4, 256, 3072], P(('grp', 'dat'), 'seq', 'head'), parts along dimension 0
- expert_hidden: bfloat16 [4, 4, 160, 8192], P('head', ('grp', 'dat'), None, 'seq'), parts along dimension 1
The draws below stay inside these ranges and needn't reach their ends.
There are 2 independent parts, one for each index of `grp`. The reference program is written for one: setup_inputs(seed, part) draws one part's arguments, and reference() takes and returns one part's arrays. A program takes and returns all parts, laid end to end along the dimension named above; an argument that names none is the same for every part. Nothing has to cross between parts.
Inputs may be any that keep to these rules, and one draw needn't show every extreme that they name: `routes`: for each sequence one expert is named by exactly 40 tokens of every aligned block of 64 positions, every other expert by at most 40 tokens of such a block; the two experts of a token differ. `sequence_lengths`: one sequence of the batch has the full length 256.
All inputs are finite; a program needn't handle non-finite values.
Results may differ from the reference program's by a relative error of at most 0.019.
Values may be sent and summed in bfloat16 or wider, within the bound.
No kernel may reach another device: no remote copies, remote signals or barrier semaphores. Data moves between devices by JAX's collectives and lax.ppermute only.
A program may use at most 128 MiB of HBM per device.

```python
import math
import jax
import jax.numpy as jnp
from jax import lax

D = 3072
QUERY_HEAD_COUNT = 24
KEY_VALUE_HEADS = 4
HEAD_SIZE = 128
EXPERTS = 4
FF = 8192
TOK_DEV = 64
MOST = 40
SEQUENCE_LENGTH = 256
SLOTS = 160
BATCH_SEQUENCES = 2
N_SEQ = 4


def draw_queries(key, part):
    array_shape = (BATCH_SEQUENCES, SEQUENCE_LENGTH, QUERY_HEAD_COUNT * HEAD_SIZE)
    draws = jnp.clip(jax.random.normal(jax.random.fold_in(key, 11), array_shape, jnp.float32), -6.0, 6.0)
    return draws.astype(jnp.bfloat16)


def draw_keys(key, part):
    array_shape = (BATCH_SEQUENCES, SEQUENCE_LENGTH, KEY_VALUE_HEADS * HEAD_SIZE)
    draws = jnp.clip(jax.random.normal(jax.random.fold_in(key, 21), array_shape, jnp.float32), -6.0, 6.0)
    return draws.astype(jnp.bfloat16)


def draw_residual_in(key, part):
    array_shape = (BATCH_SEQUENCES, SEQUENCE_LENGTH, D)
    col_frac = jnp.arange(D, dtype=jnp.float32) / D
    row_scale = jnp.exp(jax.random.uniform(jax.random.fold_in(key, 31), (BATCH_SEQUENCES, SEQUENCE_LENGTH, 1), jnp.float32, math.log(0.3), math.log(3.0)))
    col_scale = 10.0 ** (col_frac - 0.7)
    noise_part = jnp.clip(jax.random.normal(jax.random.fold_in(key, 34), array_shape, jnp.float32), -6.0, 6.0)
    values = noise_part * col_scale * row_scale
    return values.astype(jnp.bfloat16)


def block_ranks(sub_key):
    return jax.random.permutation(sub_key, TOK_DEV)


def draw_routes(key, part):
    per_row = SEQUENCE_LENGTH // TOK_DEV
    blocks = BATCH_SEQUENCES * per_row
    others = EXPERTS - 1
    hot_expert = jnp.repeat(jax.random.randint(jax.random.fold_in(key, 41), (BATCH_SEQUENCES, 1), 0, EXPERTS), per_row, axis=0)
    rank_in_block = jax.vmap(block_ranks)(jax.random.split(jax.random.fold_in(key, 42), blocks)).astype(jnp.int32)
    turn_first = jax.random.randint(jax.random.fold_in(key, 43), (blocks, 1), 0, others)
    turn_second = jax.random.randint(jax.random.fold_in(key, 44), (blocks, 1), 0, others)
    in_hot = rank_in_block < MOST
    rest = rank_in_block - MOST
    partner = (hot_expert + 1 + (rank_in_block + turn_first) % others) % EXPERTS
    first_other = (hot_expert + 1 + (rest + turn_second) % others) % EXPERTS
    second_other = (hot_expert + 1 + (rest + turn_second + 1) % others) % EXPERTS
    first_pick = jnp.where(in_hot, hot_expert, first_other)
    second = jnp.where(in_hot, partner, second_other)
    flip_order = jax.random.randint(jax.random.fold_in(key, 45), (blocks, TOK_DEV), 0, 2) == 1
    lead = jnp.where(flip_order, second, first_pick)
    trail = jnp.where(flip_order, first_pick, second)
    return jnp.stack([lead, trail], axis=-1).reshape(BATCH_SEQUENCES, SEQUENCE_LENGTH, 2).astype(jnp.int32)


def draw_sequence_lengths(key, part):
    lengths_drawn = jax.random.randint(jax.random.fold_in(key, 51), (BATCH_SEQUENCES,), SEQUENCE_LENGTH // 2, SEQUENCE_LENGTH + 1)
    full_row = jax.random.randint(jax.random.fold_in(key, 52), (), 0, BATCH_SEQUENCES)
    return jnp.where(jnp.arange(BATCH_SEQUENCES) == full_row, SEQUENCE_LENGTH, lengths_drawn).astype(jnp.int32)


def plant(values, stream_key, least, high):
    shape = values.shape
    index_at = [jax.random.randint(jax.random.fold_in(stream_key, axis), (), 0, shape[axis]) for axis in range(len(shape))]
    values = values.at[tuple(index_at)].set(least)
    longest = shape.index(max(shape))
    index_at[longest] = (index_at[longest] + 1) % shape[longest]
    return values.at[tuple(index_at)].set(high)


def level_of(own_key, extent, cuts, least, largest):
    loudness, own = 1.0, jax.random.fold_in(own_key, 6)
    for dim, blocks in cuts:
        heights = jnp.exp(jax.random.uniform(jax.random.fold_in(own, dim), (blocks,), jnp.float32, least / len(cuts), largest / len(cuts)))
        loudness = loudness * jnp.repeat(heights, extent[dim] // blocks).reshape([-1 if axis == dim else 1 for axis in range(len(extent))])
    return loudness


def gaussian(key, extent, spread, most, pieces=(), kind=jnp.bfloat16):
    values = spread * jax.random.normal(key, extent, jnp.float32)
    if pieces:
        values = values * level_of(key, extent, pieces, -0.22, 0.18)
    return jnp.clip(values, -most, most).astype(kind)


def setup_inputs(seed: int = 0, part: int = 0) -> dict:
    splits = jax.random.split(jax.random.key(seed), 12)
    own_keys = jax.random.split(jax.random.fold_in(splits[11], part), 12)
    queries = draw_queries(jax.random.fold_in(jax.random.fold_in(splits[11], part), 71), part)
    keys = draw_keys(jax.random.fold_in(jax.random.fold_in(splits[11], part), 71), part)
    values = gaussian(own_keys[2], (BATCH_SEQUENCES, SEQUENCE_LENGTH, KEY_VALUE_HEADS * HEAD_SIZE), 1.0, 6.0, ((0, 2), (1, 4), (2, 2)))
    residual_in = draw_residual_in(jax.random.fold_in(jax.random.fold_in(splits[11], part), 71), part)
    out_proj = gaussian(splits[4], (QUERY_HEAD_COUNT, HEAD_SIZE, D), HEAD_SIZE ** -0.5, 0.5, ((0, 2), (1, 4)))
    norm_gain = jnp.clip(1.0 + 0.1 * jax.random.normal(splits[5], (D,), jnp.float32), 0.5, 1.5).astype(jnp.bfloat16)
    expert_gate = gaussian(splits[6], (EXPERTS, D, FF), D ** -0.5, 0.109375, ((0, 2), (2, 4)))
    expert_up = gaussian(splits[7], (EXPERTS, D, FF), D ** -0.5, 0.109375, ((0, 2), (2, 4)))
    routes = draw_routes(jax.random.fold_in(jax.random.fold_in(splits[11], part), 71), part)
    gate_numer = plant(jax.random.randint(own_keys[9], (BATCH_SEQUENCES, SEQUENCE_LENGTH), 64, 192), jax.random.fold_in(own_keys[9], 1), 64, 191).astype(jnp.int32)
    sequence_lengths = draw_sequence_lengths(jax.random.fold_in(jax.random.fold_in(splits[11], part), 71), part)
    return dict(queries=queries, keys=keys, values=values, residual_in=residual_in, out_proj=out_proj, norm_gain=norm_gain, expert_gate=expert_gate, expert_up=expert_up, routes=routes, gate_numer=gate_numer, sequence_lengths=sequence_lengths)


EPS = 1e-05
NEG = -1e+30

def slot_sources(marked, capacity):
    tok_len = marked.shape[1]
    counted = jnp.cumsum(marked, axis=1)
    rank_ids = jnp.arange(capacity, dtype=jnp.int32)
    source = lax.optimization_barrier(jnp.sum((counted[:, None, :] <= rank_ids[None, :, None]).astype(jnp.int32), axis=2))
    filled = rank_ids[None, :] < counted[:, -1:]
    source = jnp.minimum(source, tok_len - 1).astype(jnp.int32)
    return (source, filled)

def expert_rows(rows_in, slot_gate, gate_matrix, up_matrix):
    gate_part = jnp.dot(rows_in, gate_matrix, preferred_element_type=jnp.float32)
    up_part = jnp.dot(rows_in, up_matrix, preferred_element_type=jnp.float32)
    return (slot_gate[:, None] * (jax.nn.silu(gate_part) * up_part)).astype(jnp.bfloat16)

def reference(queries, keys, values, residual_in, out_proj, norm_gain, expert_gate, expert_up, routes, gate_numer, sequence_lengths):
    heads_per_group = QUERY_HEAD_COUNT // KEY_VALUE_HEADS
    score_scale = 1.0 / math.sqrt(HEAD_SIZE)
    positions = jnp.arange(SEQUENCE_LENGTH, dtype=jnp.int32)
    grouped_queries = queries.reshape(BATCH_SEQUENCES, SEQUENCE_LENGTH, KEY_VALUE_HEADS, heads_per_group, HEAD_SIZE).transpose(0, 2, 1, 3, 4).reshape(BATCH_SEQUENCES * KEY_VALUE_HEADS, SEQUENCE_LENGTH, heads_per_group, HEAD_SIZE)
    grouped_keys = keys.reshape(BATCH_SEQUENCES, SEQUENCE_LENGTH, KEY_VALUE_HEADS, HEAD_SIZE).transpose(0, 2, 1, 3).reshape(BATCH_SEQUENCES * KEY_VALUE_HEADS, SEQUENCE_LENGTH, HEAD_SIZE)
    grouped_values = values.reshape(BATCH_SEQUENCES, SEQUENCE_LENGTH, KEY_VALUE_HEADS, HEAD_SIZE).transpose(0, 2, 1, 3).reshape(BATCH_SEQUENCES * KEY_VALUE_HEADS, SEQUENCE_LENGTH, HEAD_SIZE)
    group_bounds = jnp.repeat(sequence_lengths, KEY_VALUE_HEADS)

    def attend(inputs):
        query_block, key_block, value_block, valid_len = inputs
        scores = jnp.einsum('thd,nd->htn', query_block.astype(jnp.float32), key_block.astype(jnp.float32), precision=lax.Precision.HIGHEST) * score_scale
        allowed = (positions[None, :] <= positions[:, None]) & (positions < valid_len)[None, :]
        scores = jnp.where(allowed[None], scores, NEG)
        top_score = lax.optimization_barrier(jnp.max(scores, axis=-1, keepdims=True))
        weights = jnp.where(allowed[None], jnp.exp(scores - top_score), 0.0)
        denom_sum = lax.optimization_barrier(jnp.sum(weights, axis=-1))
        rounded = lax.optimization_barrier(weights.astype(jnp.bfloat16)).astype(jnp.float32)
        weighted = jnp.einsum('htn,nd->thd', rounded, value_block.astype(jnp.float32), precision=lax.Precision.HIGHEST)
        return (weighted / denom_sum.T[:, :, None]).astype(jnp.bfloat16)
    attended_values = lax.map(attend, (grouped_queries, grouped_keys, grouped_values, group_bounds))
    attended_values = attended_values.reshape(BATCH_SEQUENCES, KEY_VALUE_HEADS, SEQUENCE_LENGTH, heads_per_group, HEAD_SIZE).transpose(0, 2, 1, 3, 4).reshape(BATCH_SEQUENCES * SEQUENCE_LENGTH, QUERY_HEAD_COUNT * HEAD_SIZE)
    mixed_sum = jnp.dot(attended_values, out_proj.reshape(QUERY_HEAD_COUNT * HEAD_SIZE, D), preferred_element_type=jnp.float32)
    stream = (residual_in.reshape(BATCH_SEQUENCES * SEQUENCE_LENGTH, D).astype(jnp.float32) + mixed_sum).astype(jnp.bfloat16)
    as_float = stream.astype(jnp.float32)
    mean_sq = lax.optimization_barrier(jnp.mean(as_float * as_float, axis=1, keepdims=True))
    normed = (as_float * lax.rsqrt(mean_sq + EPS) * norm_gain.astype(jnp.float32)).astype(jnp.bfloat16)
    first_weight = gate_numer.astype(jnp.float32) / 256.0
    blocks = BATCH_SEQUENCES * N_SEQ

    def one_expert(inputs):
        gate_matrix, up_matrix, expert_id = inputs
        gates = jnp.where(routes[..., 0] == expert_id, first_weight, 0.0) + jnp.where(routes[..., 1] == expert_id, 1.0 - first_weight, 0.0)
        marked = (gates > 0).astype(jnp.int32).reshape(blocks, TOK_DEV)
        source, filled = slot_sources(marked, MOST)
        flat_index = (jnp.arange(blocks, dtype=jnp.int32)[:, None] * TOK_DEV + source).reshape(-1)
        rows_in = jnp.take(normed, flat_index, axis=0)
        slot_gate = jnp.where(filled.reshape(-1), jnp.take(gates.reshape(-1), flat_index), 0.0)
        return expert_rows(rows_in, slot_gate, gate_matrix, up_matrix).reshape(BATCH_SEQUENCES, SLOTS, FF)
    hidden = lax.map(one_expert, (expert_gate, expert_up, jnp.arange(EXPERTS, dtype=jnp.int32)))
    return (stream.reshape(BATCH_SEQUENCES, SEQUENCE_LENGTH, D), hidden)
```

```python
import functools
import math

import jax
import jax.numpy as jnp
from jax import lax
from jax.experimental import pallas as pl
from jax.experimental.pallas import tpu as pltpu
from jax.sharding import PartitionSpec as P

HEAD_SIZE = 128
QUERY_HEAD_COUNT = 24
KEY_VALUE_HEADS = 4
MOST = 40
EPS = 1e-05
NEG = -1e30
F32 = jnp.float32
BF16 = jnp.bfloat16

VMEM = pl.BlockSpec(memory_space=pltpu.VMEM)
SMEM = pl.BlockSpec(memory_space=pltpu.SMEM)
ANY = pl.BlockSpec(memory_space=pl.ANY)


def pairwise(count):
    return count in (1, 2, 4)


def swap(array, axis, step, upward=False):
    count = lax.axis_size(axis)
    pairs = [(i, i ^ step) for i in range(count) if not upward or i < i ^ step]
    return lax.ppermute(array, axis, pairs)


def spread(array, axis, upward=False):
    count = lax.axis_size(axis)
    if pairwise(count):
        return [array] + [swap(array, axis, k, upward) for k in range(1, count)]
    return [lax.all_gather(array, axis, axis=0, tiled=True)]


def attention_kernel(shape, info, queries, own_keys, own_values, *refs):
    tokens, groups, per_group, pieces, split = shape
    kv_refs, outs = refs[:pieces], refs[pieces:]
    rank, flip, valid_len = info[0], info[1], info[2]
    width = groups * HEAD_SIZE
    if split:
        key_parts = [own_keys[...]] + [ref[:, :width] for ref in kv_refs]
        value_parts = [own_values[...]] + [ref[:, width:] for ref in kv_refs]
    else:
        key_parts = [ref[:, :width] for ref in kv_refs]
        value_parts = [ref[:, width:] for ref in kv_refs]
    all_keys = jnp.concatenate(key_parts, axis=0)
    all_values = jnp.concatenate(value_parts, axis=0)
    length = all_keys.shape[0]
    column = lax.broadcasted_iota(jnp.int32, (tokens, length), 1)
    block = lax.div(column, tokens)
    key_pos = lax.bitwise_xor(block, flip) * tokens + (column - block * tokens)
    query_pos = rank * tokens + lax.broadcasted_iota(jnp.int32, (tokens, length), 0)
    allowed = ((key_pos <= query_pos) & (key_pos < valid_len)).astype(F32)
    allowed = jnp.concatenate([allowed] * per_group, axis=0) > 0
    scale = 1.0 / math.sqrt(HEAD_SIZE)
    attended = []
    for g in range(groups):
        heads = [g * per_group + a for a in range(per_group)]
        rows = jnp.concatenate(
            [queries[:, h * HEAD_SIZE : (h + 1) * HEAD_SIZE] for h in heads], axis=0
        )
        lanes = slice(g * HEAD_SIZE, (g + 1) * HEAD_SIZE)
        scores = (
            lax.dot_general(
                rows, all_keys[:, lanes], (((1,), (1,)), ((), ())), preferred_element_type=F32
            )
            * scale
        )
        scores = jnp.where(allowed, scores, NEG)
        top = jnp.max(scores, axis=-1, keepdims=True)
        weights = jnp.where(allowed, jnp.exp(scores - top), 0.0)
        denom = jnp.sum(weights, axis=-1, keepdims=True)
        mixed = jnp.dot(weights.astype(BF16), all_values[:, lanes], preferred_element_type=F32)
        mixed = mixed / denom
        attended += [mixed[a * tokens : (a + 1) * tokens] for a in range(per_group)]
    if not split:
        outs[0][...] = jnp.concatenate(attended, axis=1).astype(BF16)
        return
    count = len(outs)
    part = HEAD_SIZE // count
    shares = [
        jnp.concatenate([o[:, j * part : (j + 1) * part] for o in attended], axis=1).astype(BF16)
        for j in range(count)
    ]
    for k in range(count):
        chosen = shares[k]
        for s in range(1, count):
            chosen = jnp.where(rank == s, shares[s ^ k], chosen)
        outs[k][...] = chosen


def attend(info, queries, keys, values, kv_parts, count):
    tokens = queries.shape[0]
    groups = keys.shape[1] // HEAD_SIZE
    per_group = QUERY_HEAD_COUNT // KEY_VALUE_HEADS
    split = pairwise(count)
    if split:
        out_shape = [
            jax.ShapeDtypeStruct((tokens, queries.shape[1] // count), BF16) for _ in range(count)
        ]
    else:
        out_shape = [jax.ShapeDtypeStruct(queries.shape, BF16)]
    length = tokens * count
    return pl.pallas_call(
        functools.partial(
            attention_kernel, (tokens, groups, per_group, len(kv_parts), split)
        ),
        out_shape=out_shape,
        in_specs=[SMEM] + [VMEM] * (3 + len(kv_parts)),
        out_specs=[VMEM] * len(out_shape),
        compiler_params=pltpu.CompilerParams(vmem_limit_bytes=32 << 20),
        cost_estimate=pl.CostEstimate(
            flops=4 * tokens * length * queries.shape[1],
            bytes_accessed=4 * queries.size + 4 * length * keys.shape[1],
            transcendentals=tokens * length * groups * per_group,
        ),
        name="attention",
    )(info, queries, keys, values, *kv_parts)


def project_kernel(parts, pieces, keep, *refs):
    rows = [refs[m * pieces : (m + 1) * pieces] for m in range(parts)]
    weights = refs[parts * pieces : parts * pieces + parts]
    outs = refs[parts * pieces + parts :]
    total = None
    for m in range(parts):
        stacked = jnp.concatenate([ref[...] for ref in rows[m]], axis=0)
        product = jnp.dot(stacked, weights[m][...], preferred_element_type=F32)
        total = product if total is None else total + product
    at = 0
    for i, out in enumerate(outs):
        out[...] = total[at : at + out.shape[0]].astype(out.dtype)
        at += out.shape[0]


def project(rows, weights, split):
    parts, pieces = len(rows), len(rows[0])
    width = weights[0].shape[1]
    tokens = sum(p.shape[0] for p in rows[0])
    out_shape = [
        jax.ShapeDtypeStruct((p.shape[0], width), BF16 if split and i else F32)
        for i, p in enumerate(rows[0])
    ]
    flat = [p for part in rows for p in part]
    return pl.pallas_call(
        functools.partial(project_kernel, parts, pieces, split),
        out_shape=out_shape,
        in_specs=[VMEM] * (len(flat) + parts),
        out_specs=[VMEM] * pieces,
        compiler_params=pltpu.CompilerParams(vmem_limit_bytes=40 << 20),
        cost_estimate=pl.CostEstimate(
            flops=2 * tokens * width * parts * weights[0].shape[0],
            bytes_accessed=2 * parts * weights[0].size + 4 * tokens * width,
            transcendentals=0,
        ),
        name="projection",
    )(*flat, *weights)


def expert_kernel(shape, info, *refs):
    tokens, group, parts, pieces, experts, slots, chunk, depth = shape
    columns = [refs[m * pieces : (m + 1) * pieces] for m in range(parts)]
    refs = refs[parts * pieces :]
    routing, refs = refs[:pieces], refs[pieces:]
    gain, gate_hbm, up_hbm, hidden, chosen, factors, buffers, sems = refs
    flip, head = info[0], info[1]
    features = gate_hbm.shape[1]
    width = features // parts
    per_expert = gate_hbm.shape[2] // chunk
    steps = experts * per_expert

    def copies(step, slot):
        e = step // per_expert
        at = pl.ds(pl.multiple_of((step % per_expert) * chunk, chunk), chunk)
        return (
            pltpu.make_async_copy(gate_hbm.at[e, :, at], buffers.at[slot, 0], sems.at[slot, 0]),
            pltpu.make_async_copy(up_hbm.at[e, :, at], buffers.at[slot, 1], sems.at[slot, 1]),
        )

    for step in range(min(depth, steps)):
        for copy in copies(step, step):
            copy.start()

    blocks = sum(ref.shape[0] for ref in routing) // 8
    size = group * tokens
    slot_row = lax.broadcasted_iota(jnp.int32, (group * slots, size), 0)
    token_col = lax.broadcasted_iota(jnp.int32, (group * slots, size), 1)
    row_block = lax.div(slot_row, slots)
    row_rank = slot_row - row_block * slots
    col_block = lax.bitwise_xor(lax.div(token_col, tokens), flip)
    same_block = row_block == col_block
    before_row = lax.broadcasted_iota(jnp.int32, (size, size), 0)
    before_col = lax.broadcasted_iota(jnp.int32, (size, size), 1)
    before = (
        (before_row < before_col)
        & (lax.div(before_row, tokens) == lax.div(before_col, tokens))
    ).astype(BF16)
    ranks = lax.broadcasted_iota(jnp.int32, (8, size), 0)
    for g in range(blocks // group):
        if pieces > 1:
            route = jnp.concatenate([ref[...] for ref in routing], axis=1)
        else:
            route = jnp.concatenate(
                [routing[0][(g * group + b) * 8 : (g * group + b) * 8 + 8] for b in range(group)],
                axis=1,
            )
        first, second, numer = route[0:1], route[1:2], route[2:3]
        weight = numer.astype(F32) / 256.0
        gate_rows = []
        for e in range(experts):
            expert = head * experts + e
            gate_rows.append(
                jnp.where(first == expert, weight, 0.0)
                + jnp.where(second == expert, 1.0 - weight, 0.0)
            )
        marked = jnp.zeros((8, size), F32)
        for e in range(experts):
            marked = jnp.where(ranks == e, (gate_rows[e] > 0).astype(F32), marked)
        counted = jnp.dot(marked.astype(BF16), before, preferred_element_type=F32)
        pick = []
        for e in range(experts):
            hit = (
                same_block
                & (counted[e : e + 1].astype(jnp.int32) == row_rank)
                & (gate_rows[e] > 0)
            )
            pick.append(hit.astype(BF16))
            at = slice(g * group * slots, (g + 1) * group * slots)
            factors[e, at, :] = jnp.sum(
                jnp.where(hit, gate_rows[e], 0.0), axis=1, keepdims=True
            )
        picks = jnp.concatenate(pick, axis=0)
        values = []
        squares = None
        for m in range(parts):
            if pieces > 1:
                raw = jnp.concatenate([ref[...] for ref in columns[m]], axis=0)
            else:
                raw = columns[m][0][g * size : (g + 1) * size]
            raw = raw.astype(F32)
            part = jnp.sum(raw * raw, axis=1, keepdims=True)
            squares = part if squares is None else squares + part
            values.append(raw)
        scale = lax.rsqrt(squares / features + EPS)
        for m in range(parts):
            place = lax.bitwise_xor(head, m)
            normed = (values[m] * scale * gain[place].astype(F32)).astype(BF16)
            rows = jnp.dot(picks, normed, preferred_element_type=F32).astype(BF16)
            for e in range(experts):
                at = slice(g * group * slots, (g + 1) * group * slots)
                chosen[place, e, at, :] = rows[e * group * slots : (e + 1) * group * slots]

    @pl.loop(0, steps)
    def _(step):
        slot = lax.rem(step, depth)
        e = step // per_expert
        for copy in copies(step, slot):
            copy.wait()
        gate_part = up_part = None
        for p in range(parts):
            at = slice(p * width, (p + 1) * width)
            rows = chosen[p, e]
            a = jnp.dot(rows, buffers[slot, 0, at, :], preferred_element_type=F32)
            b = jnp.dot(rows, buffers[slot, 1, at, :], preferred_element_type=F32)
            gate_part = a if gate_part is None else gate_part + a
            up_part = b if up_part is None else up_part + b
        result = factors[e] * (gate_part / (1.0 + jnp.exp(-gate_part)) * up_part)
        at = pl.ds(pl.multiple_of((step % per_expert) * chunk, chunk), chunk)
        hidden[e, :, at] = result.astype(BF16)

        @pl.when(step + depth < steps)
        def _():
            for copy in copies(step + depth, slot):
                copy.start()


def run_experts(info, columns, routing, gain, expert_gate, expert_up, tokens, count):
    parts, pieces = len(columns), len(routing)
    experts, features, hidden_units = expert_gate.shape
    group = min(4, count)
    chunk = min(512, hidden_units)
    steps = experts * (hidden_units // chunk)
    depth = min(4, steps)
    slots = MOST * count
    shape = (tokens, group, parts, pieces, experts, MOST, chunk, depth)
    flat = [p for part in columns for p in part]
    return pl.pallas_call(
        functools.partial(expert_kernel, shape),
        out_shape=jax.ShapeDtypeStruct((experts, slots, hidden_units), BF16),
        in_specs=[SMEM] + [VMEM] * (len(flat) + pieces + 1) + [ANY, ANY],
        out_specs=VMEM,
        scratch_shapes=[
            pltpu.VMEM((parts, experts, slots, features // parts), BF16),
            pltpu.VMEM((experts, slots, 1), F32),
            pltpu.VMEM((depth, 2, features, chunk), BF16),
            pltpu.SemaphoreType.DMA((depth, 2)),
        ],
        compiler_params=pltpu.CompilerParams(vmem_limit_bytes=56 << 20),
        cost_estimate=pl.CostEstimate(
            flops=4 * experts * slots * features * hidden_units,
            bytes_accessed=4 * expert_gate.size,
            transcendentals=experts * slots * hidden_units,
        ),
        name="experts",
    )(info, *flat, *routing, gain, expert_gate, expert_up)


def local(
    queries,
    keys,
    values,
    residual_in,
    out_proj,
    norm_gain,
    expert_gate,
    expert_up,
    routes,
    gate_numer,
    sequence_lengths,
):
    tokens = queries.shape[1]
    count = lax.axis_size("seq")
    head_count = lax.axis_size("head")
    seq_rank = lax.axis_index("seq")
    head_rank = lax.axis_index("head")
    split = pairwise(count)
    flip = seq_rank if split else jnp.zeros_like(seq_rank)
    share = residual_in.shape[2]
    features = out_proj.shape[2]
    heads, part, _ = out_proj.shape

    own_kv = jnp.concatenate([keys[0], values[0]], axis=1)
    kv_parts = spread(own_kv, "seq", upward=True)
    if split:
        kv_parts = kv_parts[1:]

    matrix = out_proj.reshape(heads * part, features)

    def columns_of(rank):
        return lax.dynamic_slice_in_dim(matrix, rank * share, share, 1)

    weights = [columns_of(head_rank)] + [
        swap(columns_of(lax.bitwise_xor(head_rank, m)), "head", m) for m in range(1, head_count)
    ]

    routing = jnp.concatenate(
        [routes[0].T, gate_numer, jnp.zeros((5, tokens), jnp.int32)], axis=0
    )
    routing = spread(routing, "seq")

    info = jnp.stack([seq_rank, flip, sequence_lengths[0]]).astype(jnp.int32)
    attended = attend(info, queries[0], keys[0], values[0], kv_parts, count)
    if split:
        attended = [attended[0]] + [swap(attended[k], "seq", k) for k in range(1, count)]
    else:
        shares = attended[0].reshape(tokens, heads, count, part).transpose(2, 0, 1, 3)
        shares = shares.reshape(count * tokens, heads * part)
        attended = [lax.all_to_all(shares, "seq", 0, 0, tiled=True)]
    rows = [attended] + [
        [swap(piece, "head", m) for piece in attended] for m in range(1, head_count)
    ]
    sums = project(rows, weights, split)
    if split:
        mixed = sums[0]
        for k in range(1, count):
            mixed = mixed + swap(sums[k], "seq", k).astype(F32)
    else:
        mixed = lax.psum_scatter(sums[0], "seq", scatter_dimension=0, tiled=True)
    stream = (residual_in[0].astype(F32) + mixed).astype(BF16)

    own_columns = spread(stream, "seq")
    columns = [own_columns] + [
        [swap(piece, "head", m) for piece in own_columns] for m in range(1, head_count)
    ]
    gain = norm_gain.reshape(head_count, 1, share)
    place = jnp.stack([flip, head_rank]).astype(jnp.int32)
    hidden = run_experts(place, columns, routing, gain, expert_gate, expert_up, tokens, count)
    return (stream[None], hidden[:, None])


def solution(mesh):
    in_specs = (
        P(("grp", "dat"), "seq", "head"),
        P(("grp", "dat"), "seq", "head"),
        P(("grp", "dat"), "seq", "head"),
        P(("grp", "dat"), "seq", "head"),
        P("head", "seq", None),
        P(),
        P("head", None, "seq"),
        P("head", None, "seq"),
        P(("grp", "dat"), "seq", None),
        P(("grp", "dat"), "seq"),
        P(("grp", "dat")),
    )
    out_specs = (P(("grp", "dat"), "seq", "head"), P("head", ("grp", "dat"), None, "seq"))
    return jax.shard_map(local, mesh=mesh, in_specs=in_specs, out_specs=out_specs, check_vma=False)
```

```python
import functools
import math

import jax
import jax.numpy as jnp
from jax import lax
from jax.experimental import pallas as pl
from jax.experimental.pallas import tpu as pltpu
from jax.sharding import PartitionSpec as P

HEAD_SIZE = 128
QUERY_HEAD_COUNT = 24
KEY_VALUE_HEADS = 4
MOST = 40
EXTRA = 16
EPS = 1e-05
NEG = -1e30
F32 = jnp.float32
BF16 = jnp.bfloat16

VMEM = pl.BlockSpec(memory_space=pltpu.VMEM)
SMEM = pl.BlockSpec(memory_space=pltpu.SMEM)
ANY = pl.BlockSpec(memory_space=pl.ANY)
place = pltpu.with_memory_space_constraint
HBM = pl.BlockSpec(memory_space=pltpu.HBM)


def pairwise(count):
    return count in (1, 2, 4)


def swap(array, axis, step, upward=False):
    count = lax.axis_size(axis)
    pairs = [(i, i ^ step) for i in range(count) if not upward or i < i ^ step]
    return lax.ppermute(array, axis, pairs)


def steps_of(count):
    return [k for k in (2, 3, 1) if k < count]


def shuffled(pieces):
    return [pieces[k] for k in (0, 2, 3, 1)] if len(pieces) == 4 else list(pieces)


def sorted_back(pieces):
    return [pieces[k] for k in (0, 3, 1, 2)] if len(pieces) == 4 else list(pieces)


def swaps(arrays, axis, upward=False):
    got = {k: swap(arrays[k], axis, k, upward) for k in steps_of(len(arrays))}
    return [arrays[0]] + [got[k] for k in range(1, len(arrays))]


def spread(array, axis, upward=False):
    count = lax.axis_size(axis)
    if pairwise(count):
        return swaps([array] * count, axis, upward)
    return [lax.all_gather(array, axis, axis=0, tiled=True)]


def attention_kernel(shape, info, queries, gain_in, routes, numer, *refs):
    tokens, groups, per_group, pieces, carried, split = shape
    kv_refs, refs = refs[:pieces], refs[pieces:]
    carried_in, refs = refs[:carried], refs[carried:]
    gain_out, carried_out, refs = refs[0], refs[1 : 1 + carried], refs[1 + carried :]
    outs, sems = refs[:-1], refs[-1]
    copies = [
        pltpu.make_async_copy(source, out, sems.at[i])
        for i, (source, out) in enumerate(zip(carried_in, carried_out))
    ]
    for copy in copies:
        copy.start()
    gain_out[...] = gain_in[...]
    rank, flip, valid_len = info[0], info[1], info[2]
    width = groups * HEAD_SIZE
    key_parts = [ref[:, :width] for ref in kv_refs]
    value_parts = [ref[:, width:] for ref in kv_refs]
    all_keys = jnp.concatenate(key_parts, axis=0)
    all_values = jnp.concatenate(value_parts, axis=0)
    length = all_keys.shape[0]
    column = lax.broadcasted_iota(jnp.int32, (tokens, length), 1)
    block = lax.div(column, tokens)
    key_pos = lax.bitwise_xor(block, flip) * tokens + (column - block * tokens)
    query_pos = rank * tokens + lax.broadcasted_iota(jnp.int32, (tokens, length), 0)
    allowed = ((key_pos <= query_pos) & (key_pos < valid_len)).astype(F32)
    allowed = jnp.concatenate([allowed] * per_group, axis=0) > 0
    scale = 1.0 / math.sqrt(HEAD_SIZE)
    attended = []
    for g in range(groups):
        heads = [g * per_group + a for a in range(per_group)]
        rows = jnp.concatenate(
            [queries[:, h * HEAD_SIZE : (h + 1) * HEAD_SIZE] for h in heads], axis=0
        )
        lanes = slice(g * HEAD_SIZE, (g + 1) * HEAD_SIZE)
        scores = (
            lax.dot_general(
                rows, all_keys[:, lanes], (((1,), (1,)), ((), ())), preferred_element_type=F32
            )
            * scale
        )
        scores = jnp.where(allowed, scores, NEG)
        top = jnp.max(scores, axis=-1, keepdims=True)
        weights = jnp.where(allowed, jnp.exp(scores - top), 0.0)
        denom = jnp.sum(weights, axis=-1, keepdims=True)
        mixed = jnp.dot(weights.astype(BF16), all_values[:, lanes], preferred_element_type=F32)
        mixed = mixed / denom
        attended += [mixed[a * tokens : (a + 1) * tokens] for a in range(per_group)]
    if not split:
        outs[0][...] = jnp.concatenate(attended, axis=1).astype(BF16)
        for copy in copies:
            copy.wait()
        return
    count = len(outs)
    part = HEAD_SIZE // count
    shares = [
        jnp.concatenate([o[:, j * part : (j + 1) * part] for o in attended], axis=1).astype(BF16)
        for j in range(count)
    ]
    routing = jnp.concatenate(
        [routes[...], numer[...], jnp.zeros((EXTRA - 3, tokens), jnp.int32)], axis=0
    )
    routing = routing.astype(F32).astype(BF16)
    for k in range(count):
        chosen = shares[k]
        for s in range(1, count):
            chosen = jnp.where(rank == s, shares[s ^ k], chosen)
        outs[k][:tokens, :] = chosen
        outs[k][tokens:, :] = jnp.zeros((EXTRA, chosen.shape[1]), BF16)
        outs[k][tokens:, :tokens] = routing
    for copy in copies:
        copy.wait()


def attend(info, queries, gain, routes, numer, kv_parts, carried, count):
    tokens = queries.shape[0]
    groups = kv_parts[0].shape[1] // (2 * HEAD_SIZE)
    per_group = QUERY_HEAD_COUNT // KEY_VALUE_HEADS
    split = pairwise(count)
    if split:
        out_shape = [
            jax.ShapeDtypeStruct((tokens + EXTRA, queries.shape[1] // count), BF16)
            for _ in range(count)
        ]
    else:
        out_shape = [jax.ShapeDtypeStruct(queries.shape, BF16)]
    length = tokens * count
    limit = min(40 << 20, (4 << 20) + 48 * per_group * tokens * length)
    out_shape = [
        jax.ShapeDtypeStruct(array.shape, BF16) for array in (gain, *carried)
    ] + out_shape
    return pl.pallas_call(
        functools.partial(
            attention_kernel, (tokens, groups, per_group, len(kv_parts), len(carried), split)
        ),
        out_shape=out_shape,
        in_specs=[SMEM] + [VMEM] * (4 + len(kv_parts)) + [ANY] * len(carried),
        out_specs=[VMEM] * len(out_shape),
        scratch_shapes=[pltpu.SemaphoreType.DMA((max(1, len(carried)),))],
        compiler_params=pltpu.CompilerParams(vmem_limit_bytes=limit),
        cost_estimate=pl.CostEstimate(
            flops=4 * tokens * length * queries.shape[1],
            bytes_accessed=4 * queries.size + 4 * length * kv_parts[0].shape[1],
            transcendentals=tokens * length * groups * per_group,
        ),
        name="attention",
    )(info, queries, gain, routes, numer, *kv_parts, *carried)


def prepare_kernel(parts, info, matrix, queries, keys, values, routes, numer, *refs):
    kv, rows, first_routes, weights = refs[:4]
    columns, sems = refs[4:-1], refs[-1]
    height, share = columns[-1].shape
    width = keys.shape[1]
    pairs = [
        (keys, kv.at[:, :width]),
        (values, kv.at[:, width:]),
        (queries, rows),
        (routes, first_routes),
        (numer, weights),
    ]
    for m, out in enumerate(columns):
        at = pl.multiple_of(lax.bitwise_xor(info[3], m) * share, share)
        lanes = pl.ds(at, share)
        if out.shape[0] == matrix.shape[0]:
            source = matrix.at[:, lanes]
        else:
            source = matrix.at[pl.ds(pl.multiple_of(info[4] * height, height), height), lanes]
        pairs.insert(2 if m else 5, (source, out))
    copies = [pltpu.make_async_copy(*pair, sems.at[i]) for i, pair in enumerate(pairs)]
    for copy in copies:
        copy.start()
    for copy in copies:
        copy.wait()


def prepare(info, matrix, queries, keys, values, routes, numer, head_count, halves):
    rows, features = matrix.shape
    tokens = queries.shape[0]
    share = features // head_count
    out_shape = [
        jax.ShapeDtypeStruct((tokens, 2 * keys.shape[1]), BF16),
        jax.ShapeDtypeStruct(queries.shape, BF16),
        jax.ShapeDtypeStruct(routes.shape, jnp.int32),
        jax.ShapeDtypeStruct(numer.shape, jnp.int32),
        jax.ShapeDtypeStruct((rows, share), BF16),
    ] + [pltpu.VMEM((rows // halves, share), BF16)] * (head_count - 1)
    sources = [matrix, queries, keys, values, routes, numer]
    return pl.pallas_call(
        functools.partial(prepare_kernel, head_count),
        out_shape=out_shape,
        in_specs=[SMEM] + [HBM] * len(sources),
        out_specs=[VMEM] * len(out_shape),
        scratch_shapes=[pltpu.SemaphoreType.DMA((5 + head_count,))],
        compiler_params=pltpu.CompilerParams(vmem_limit_bytes=8 << 20),
        cost_estimate=pl.CostEstimate(
            flops=0, bytes_accessed=4 * rows * features, transcendentals=0
        ),
        name="prepare",
    )(info, *[place(source, pltpu.HBM) for source in sources])


def project_kernel(parts, pieces, tokens, halves, info, *refs):
    rows = [sorted_back(refs[m * pieces : (m + 1) * pieces]) for m in range(parts)]
    refs = refs[parts * pieces :]
    weights = [refs[0][...]]
    refs = refs[1:]
    for m in range(1, parts):
        if halves == 1:
            weights.append(refs[0][...])
        else:
            mine, other = refs[0][...], refs[1][...]
            first = info[4] == 0
            weights += [jnp.where(first, mine, other), jnp.where(first, other, mine)]
        refs = refs[halves:]
    weights = jnp.concatenate(weights, axis=0)
    outs = refs
    if tokens:
        route, outs = outs[0], outs[1:]
        route[...] = jnp.concatenate([ref[tokens : tokens + 8, :tokens] for ref in rows[0]], axis=1)
    total = None
    depth = rows[0][0].shape[1]
    for m in range(parts):
        stacked = jnp.concatenate([ref[: tokens or ref.shape[0]] for ref in rows[m]], axis=0)
        product = jnp.dot(
            stacked, weights[m * depth : (m + 1) * depth], preferred_element_type=F32
        )
        total = product if total is None else total + product
    at = 0
    for i, out in enumerate(outs):
        out[...] = total[at : at + out.shape[0]].astype(out.dtype)
        at += out.shape[0]


def project(info, rows, weights, each):
    parts, pieces = len(rows), len(rows[0])
    depth, width = weights[0][0].shape
    flat_weights = [w for part in weights for w in part]
    heights = [each or p.shape[0] for p in rows[0]]
    tokens = sum(heights)
    out_shape = [
        jax.ShapeDtypeStruct((h, width), BF16 if each and i else F32)
        for i, h in enumerate(heights)
    ]
    if each:
        out_shape = [jax.ShapeDtypeStruct((8, tokens), BF16)] + out_shape
    flat = [p for part in rows for p in shuffled(part)]
    return pl.pallas_call(
        functools.partial(project_kernel, parts, pieces, each, len(weights[-1])),
        out_shape=out_shape,
        in_specs=[SMEM] + [VMEM] * (len(flat) + len(flat_weights)),
        out_specs=[VMEM] * len(out_shape),
        compiler_params=pltpu.CompilerParams(vmem_limit_bytes=min(40 << 20, (4 << 20) + 16 * tokens * width)),
        cost_estimate=pl.CostEstimate(
            flops=2 * tokens * width * parts * depth,
            bytes_accessed=2 * parts * depth * width + 4 * tokens * width,
            transcendentals=0,
        ),
        name="projection",
    )(info, *flat, *flat_weights)


def fetch_kernel(chunk, gate_hbm, up_hbm, after, *refs):
    outs, done, sems = refs[:-2], refs[-2], refs[-1]
    per_expert = gate_hbm.shape[2] // chunk
    copies = []
    for step, out in enumerate(outs):
        at = pl.ds((step % per_expert) * chunk, chunk)
        for i, source in enumerate((gate_hbm, up_hbm)):
            copies.append(
                pltpu.make_async_copy(
                    source.at[step // per_expert, :, at], out.at[i], sems.at[step, i]
                )
            )
    for copy in copies:
        copy.start()
    done[...] = jnp.zeros_like(done)
    for copy in copies:
        copy.wait()


def fetch(expert_gate, expert_up, after, chunk, early):
    features = expert_gate.shape[1]
    return pl.pallas_call(
        functools.partial(fetch_kernel, chunk),
        out_shape=[pltpu.VMEM((2, features, chunk), BF16)] * early
        + [
            jax.ShapeDtypeStruct((8, 128), F32),
        ],
        in_specs=[HBM, HBM, ANY],
        out_specs=[VMEM] * (early + 1),
        scratch_shapes=[pltpu.SemaphoreType.DMA((early, 2))],
        compiler_params=pltpu.CompilerParams(vmem_limit_bytes=1 << 20),
        cost_estimate=pl.CostEstimate(
            flops=0, bytes_accessed=8 * early * features * chunk, transcendentals=0
        ),
        name="fetch",
    )(place(expert_gate, pltpu.HBM), place(expert_up, pltpu.HBM), after)


def add_kernel(residual, own, *refs):
    total = residual[...].astype(F32) + own[...]
    for ref in refs[:-3]:
        total = total + ref[...].astype(F32)
    refs[-2][...] = total.astype(BF16)
    refs[-1][...] = total.astype(BF16)


def add(residual, own, received, after):
    return pl.pallas_call(
        add_kernel,
        out_shape=[jax.ShapeDtypeStruct(residual.shape, BF16)] * 2,
        in_specs=[VMEM] * (2 + len(received)) + [ANY],
        out_specs=[VMEM] * 2,
        compiler_params=pltpu.CompilerParams(vmem_limit_bytes=8 << 20),
        name="add",
    )(residual, own, *received, after)


def expert_kernel(shape, info, *refs):
    tokens, group, parts, pieces, experts, slots, chunk, depth, early = shape
    columns = [sorted_back(refs[m * pieces : (m + 1) * pieces]) for m in range(parts)]
    refs = refs[parts * pieces :]
    routing, gain, refs = refs[0], refs[1], refs[2:]
    fetched, refs = refs[:early], refs[early:]
    gate_hbm, up_hbm, hidden, chosen, factors, buffers, sems = refs
    flip, head = info[1], info[3]
    features = gate_hbm.shape[1]
    width = features // parts
    per_expert = gate_hbm.shape[2] // chunk
    steps = experts * per_expert

    def copies(step, slot):
        e = step // per_expert
        at = pl.ds(pl.multiple_of((step % per_expert) * chunk, chunk), chunk)
        return (
            pltpu.make_async_copy(gate_hbm.at[e, :, at], buffers.at[slot, 0], sems.at[slot, 0]),
            pltpu.make_async_copy(up_hbm.at[e, :, at], buffers.at[slot, 1], sems.at[slot, 1]),
        )

    for slot in range(depth):
        for copy in copies(early + slot, slot):
            copy.start()

    blocks = routing.shape[1] // tokens
    size = group * tokens
    slot_row = lax.broadcasted_iota(jnp.int32, (group * slots, size), 0)
    token_col = lax.broadcasted_iota(jnp.int32, (group * slots, size), 1)
    row_block = lax.div(slot_row, slots)
    row_rank = slot_row - row_block * slots
    col_block = lax.bitwise_xor(lax.div(token_col, tokens), flip)
    same_block = row_block == col_block
    before_row = lax.broadcasted_iota(jnp.int32, (size, size), 0)
    before_col = lax.broadcasted_iota(jnp.int32, (size, size), 1)
    before = (
        (before_row < before_col)
        & (lax.div(before_row, tokens) == lax.div(before_col, tokens))
    ).astype(BF16)
    ranks = lax.broadcasted_iota(jnp.int32, (8, size), 0)
    for g in range(blocks // group):
        route = routing[:, g * size : (g + 1) * size].astype(F32)
        first, second, numer = route[0:1], route[1:2], route[2:3]
        weight = numer / 256.0
        gate_rows = []
        for e in range(experts):
            expert = (head * experts + e).astype(F32)
            gate_rows.append(
                jnp.where(first == expert, weight, 0.0)
                + jnp.where(second == expert, 1.0 - weight, 0.0)
            )
        marked = jnp.zeros((8, size), F32)
        for e in range(experts):
            marked = jnp.where(ranks == e, (gate_rows[e] > 0).astype(F32), marked)
        counted = jnp.dot(marked.astype(BF16), before, preferred_element_type=F32)
        at = slice(g * group * slots, (g + 1) * group * slots)
        pick = []
        for e in range(experts):
            hit = (
                same_block
                & (counted[e : e + 1].astype(jnp.int32) == row_rank)
                & (gate_rows[e] > 0)
            )
            pick.append(hit.astype(BF16))
            factors[e, at, :] = jnp.sum(jnp.where(hit, gate_rows[e], 0.0), axis=1, keepdims=True)
        picks = jnp.concatenate(pick, axis=0)

        def stream_part(m):
            if pieces > 1:
                return jnp.concatenate([ref[...] for ref in columns[m]], axis=0).astype(F32)
            return columns[m][0][g * size : (g + 1) * size].astype(F32)

        squares = None
        for m in range(parts):
            raw = stream_part(m)
            part = jnp.sum(raw * raw, axis=1, keepdims=True)
            squares = part if squares is None else squares + part
        scale = lax.rsqrt(squares / features + EPS)
        for m in range(parts):
            part_at = lax.bitwise_xor(head, m)
            normed = (stream_part(m) * scale * gain[part_at].astype(F32)).astype(BF16)
            rows = jnp.dot(picks, normed, preferred_element_type=F32).astype(BF16)
            for e in range(experts):
                chosen[part_at, e, at, :] = rows[e * group * slots : (e + 1) * group * slots]

    def compute(step, weights):
        e = step // per_expert
        gate_part = up_part = None
        for p in range(parts):
            at = slice(p * width, (p + 1) * width)
            rows = chosen[p, e]
            a = jnp.dot(rows, weights[0, at, :], preferred_element_type=F32)
            b = jnp.dot(rows, weights[1, at, :], preferred_element_type=F32)
            gate_part = a if gate_part is None else gate_part + a
            up_part = b if up_part is None else up_part + b
        result = factors[e] * (gate_part / (1.0 + jnp.exp(-gate_part)) * up_part)
        at = pl.ds(pl.multiple_of((step % per_expert) * chunk, chunk), chunk)
        hidden[e, :, at] = result.astype(BF16)

    for step in range(early):
        compute(step, fetched[step])

    if depth:

        @pl.loop(early, steps)
        def _(step):
            slot = lax.rem(step - early, depth)
            for copy in copies(step, slot):
                copy.wait()
            compute(step, buffers.at[slot])

            @pl.when(step + depth < steps)
            def _():
                for copy in copies(step + depth, slot):
                    copy.start()


def run_experts(info, columns, routing, gain, fetched, expert_gate, expert_up, tokens, count):
    parts, pieces = len(columns), len(columns[0])
    experts, features, hidden_units = expert_gate.shape
    early, chunk = len(fetched), fetched[0].shape[2]
    late = experts * (hidden_units // chunk) - early
    depth = min(1, late)
    slots = MOST * count
    shape = (tokens, min(4, count), parts, pieces, experts, MOST, chunk, depth, early)
    flat = [p for part in columns for p in shuffled(part)]
    limit = (12 << 20) if late else (40 << 20)
    return pl.pallas_call(
        functools.partial(expert_kernel, shape),
        out_shape=jax.ShapeDtypeStruct((experts, slots, hidden_units), BF16),
        in_specs=[SMEM] + [VMEM] * (len(flat) + 2 + early) + [HBM, HBM],
        out_specs=VMEM,
        scratch_shapes=[
            pltpu.VMEM((parts, experts, slots, features // parts), BF16),
            pltpu.VMEM((experts, slots, 1), F32),
            pltpu.VMEM((max(depth, 1), 2, features, chunk), BF16),
            pltpu.SemaphoreType.DMA((max(depth, 1), 2)),
        ],
        compiler_params=pltpu.CompilerParams(vmem_limit_bytes=limit),
        cost_estimate=pl.CostEstimate(
            flops=4 * experts * slots * features * hidden_units,
            bytes_accessed=2 * expert_gate.size,
            transcendentals=experts * slots * hidden_units,
        ),
        name="experts",
    )(
        info,
        *flat,
        routing,
        gain,
        *[place(part, pltpu.VMEM) for part in fetched],
        place(expert_gate, pltpu.HBM),
        place(expert_up, pltpu.HBM),
    )


def local(
    queries,
    keys,
    values,
    residual_in,
    out_proj,
    norm_gain,
    expert_gate,
    expert_up,
    routes,
    gate_numer,
    sequence_lengths,
):
    tokens = queries.shape[1]
    count = lax.axis_size("seq")
    head_count = lax.axis_size("head")
    seq_rank = lax.axis_index("seq")
    head_rank = lax.axis_index("head")
    split = pairwise(count)
    flip = seq_rank if split else jnp.zeros_like(seq_rank)
    share = residual_in.shape[2]
    features = out_proj.shape[2]
    heads, part, _ = out_proj.shape

    info = jnp.stack([seq_rank, flip, sequence_lengths[0], head_rank, lax.axis_index("dat")])
    info = info.astype(jnp.int32)
    matrix = out_proj.reshape(heads * part, features)
    halves = 2 if lax.axis_size("dat") == 2 and matrix.shape[0] % 32 == 0 else 1
    own_kv, rows, own_routes, numer, own_weights, *weights = prepare(
        info, matrix, queries[0], keys[0], values[0], routes[0].T, gate_numer, head_count, halves
    )

    weights = [swap(weights[m - 1], "head", m) for m in range(1, head_count)]

    kv_parts = spread(own_kv, "seq", upward=True)
    gain = norm_gain.reshape(head_count, 1, share)

    gain, *attended = attend(
        info, rows, gain, own_routes, numer, kv_parts, weights if halves == 2 else [], count
    )
    if halves == 2:
        carried, attended = attended[: head_count - 1], attended[head_count - 1 :]
        weights = [[got, swap(again, "dat", 1)] for got, again in zip(weights, carried)]
    else:
        weights = [[got] for got in weights]
    weights = [[own_weights]] + weights
    if split:
        attended = swaps(attended, "seq")
    else:
        shares = attended[0].reshape(tokens, heads, count, part).transpose(2, 0, 1, 3)
        shares = shares.reshape(count * tokens, heads * part)
        attended = [lax.all_to_all(shares, "seq", 0, 0, tiled=True)]
        routing = jnp.concatenate(
            [own_routes, numer, jnp.zeros((5, tokens), jnp.int32)], axis=0
        )
        routing = lax.all_gather(routing, "seq", axis=1, tiled=True)
    rows = [attended] + [
        [swap(piece, "head", m) for piece in attended] for m in range(1, head_count)
    ]
    sums = project(info, rows, weights, tokens if split else 0)
    if split:
        routing, *sums = sums
    chunk = min(512, expert_gate.shape[2])
    early = max(1, expert_gate.shape[0] * (expert_gate.shape[2] // chunk) * 12 // 16)
    *fetched, done = fetch(expert_gate, expert_up, sums[-1], chunk, early)
    if split:
        received = swaps(sums, "seq")[1:]
        stream, shared = add(residual_in[0], sums[0], received, done)
    else:
        mixed = lax.psum_scatter(sums[0], "seq", scatter_dimension=0, tiled=True)
        stream, shared = add(residual_in[0], mixed, [], done)

    own_columns = spread(shared, "seq")
    columns = [own_columns] + [
        [swap(piece, "head", m) for piece in own_columns] for m in range(1, head_count)
    ]
    hidden = run_experts(
        info, columns, routing, gain, fetched, expert_gate, expert_up, tokens, count
    )
    return (stream[None], hidden[:, None])


def solution(mesh):
    in_specs = (
        P(("grp", "dat"), "seq", "head"),
        P(("grp", "dat"), "seq", "head"),
        P(("grp", "dat"), "seq", "head"),
        P(("grp", "dat"), "seq", "head"),
        P("head", "seq", None),
        P(),
        P("head", None, "seq"),
        P("head", None, "seq"),
        P(("grp", "dat"), "seq", None),
        P(("grp", "dat"), "seq"),
        P(("grp", "dat")),
    )
    out_specs = (P(("grp", "dat"), "seq", "head"), P("head", ("grp", "dat"), None, "seq"))
    return jax.shard_map(local, mesh=mesh, in_specs=in_specs, out_specs=out_specs, check_vma=False)
```

```python
import functools
import math

import jax
import jax.numpy as jnp
from jax import lax
from jax.experimental import pallas as pl
from jax.experimental.pallas import tpu as pltpu
from jax.sharding import PartitionSpec as P

HEAD_SIZE = 128
QUERY_HEAD_COUNT = 24
KEY_VALUE_HEADS = 4
MOST = 40
EXTRA = 16
ATTENDED_ORDER = (0, 1, 2, 3)
STREAM_ORDER = (0, 3, 1, 2)
EPS = 1e-05
NEG = -1e30
F32 = jnp.float32
BF16 = jnp.bfloat16

VMEM = pl.BlockSpec(memory_space=pltpu.VMEM)
SMEM = pl.BlockSpec(memory_space=pltpu.SMEM)
ANY = pl.BlockSpec(memory_space=pl.ANY)
place = pltpu.with_memory_space_constraint
HBM = pl.BlockSpec(memory_space=pltpu.HBM)


def pairwise(count):
    return count in (1, 2, 4)


def swap(array, axis, step, upward=False):
    count = lax.axis_size(axis)
    pairs = [(i, i ^ step) for i in range(count) if not upward or i < i ^ step]
    return lax.ppermute(array, axis, pairs)


def steps_of(count):
    return [k for k in (2, 3, 1) if k < count]


def shuffled(pieces, order):
    return [pieces[k] for k in order] if len(pieces) == len(order) else list(pieces)


def sorted_back(pieces, order):
    return [pieces[order.index(k)] for k in range(4)] if len(pieces) == len(order) else list(pieces)


def swaps(arrays, axis, upward=False):
    got = {k: swap(arrays[k], axis, k, upward) for k in steps_of(len(arrays))}
    return [arrays[0]] + [got[k] for k in range(1, len(arrays))]


def spread(array, axis, upward=False):
    count = lax.axis_size(axis)
    if pairwise(count):
        return swaps([array] * count, axis, upward)
    return [lax.all_gather(array, axis, axis=0, tiled=True)]


def attention_kernel(shape, lengths, matrix, queries, gain_in, routes, numer, *refs):
    tokens, groups, per_group, pieces, carried, split = shape
    kv_refs, refs = refs[:pieces], refs[pieces:]
    carried_in, refs = refs[:carried], refs[carried:]
    own, gain_out, refs = refs[0], refs[1], refs[2:]
    carried_out, refs = refs[:carried], refs[carried:]
    outs, sems = refs[:-1], refs[-1]
    rank = lax.axis_index("seq")
    share = own.shape[1]
    lanes = pl.ds(pl.multiple_of(lax.axis_index("head") * share, share), share)
    pairs = [(matrix.at[:, lanes], own), *zip(carried_in, carried_out)]
    copies = [pltpu.make_async_copy(*pair, sems.at[i]) for i, pair in enumerate(pairs)]
    for copy in copies:
        copy.start()
    gain_out[...] = gain_in[...]
    flip, valid_len = rank if split else 0, lengths[0]
    width = groups * HEAD_SIZE
    key_parts = [ref[:, :width] for ref in kv_refs]
    value_parts = [ref[:, width:] for ref in kv_refs]
    all_keys = jnp.concatenate(key_parts, axis=0)
    all_values = jnp.concatenate(value_parts, axis=0)
    length = all_keys.shape[0]
    column = lax.broadcasted_iota(jnp.int32, (tokens, length), 1)
    block = lax.div(column, tokens)
    key_pos = lax.bitwise_xor(block, flip) * tokens + (column - block * tokens)
    query_pos = rank * tokens + lax.broadcasted_iota(jnp.int32, (tokens, length), 0)
    allowed = ((key_pos <= query_pos) & (key_pos < valid_len)).astype(F32)
    allowed = jnp.concatenate([allowed] * per_group, axis=0) > 0
    scale = 1.0 / math.sqrt(HEAD_SIZE)
    attended = []
    for g in range(groups):
        heads = [g * per_group + a for a in range(per_group)]
        rows = jnp.concatenate(
            [queries[:, h * HEAD_SIZE : (h + 1) * HEAD_SIZE] for h in heads], axis=0
        )
        lanes = slice(g * HEAD_SIZE, (g + 1) * HEAD_SIZE)
        scores = (
            lax.dot_general(
                rows, all_keys[:, lanes], (((1,), (1,)), ((), ())), preferred_element_type=F32
            )
            * scale
        )
        scores = jnp.where(allowed, scores, NEG)
        top = jnp.max(scores, axis=-1, keepdims=True)
        weights = jnp.where(allowed, jnp.exp(scores - top), 0.0)
        denom = jnp.sum(weights, axis=-1, keepdims=True)
        mixed = jnp.dot(weights.astype(BF16), all_values[:, lanes], preferred_element_type=F32)
        mixed = mixed / denom
        attended += [mixed[a * tokens : (a + 1) * tokens] for a in range(per_group)]
    if not split:
        outs[0][...] = jnp.concatenate(attended, axis=1).astype(BF16)
        for copy in copies:
            copy.wait()
        return
    count = len(outs)
    part = HEAD_SIZE // count
    shares = [
        jnp.concatenate([o[:, j * part : (j + 1) * part] for o in attended], axis=1).astype(BF16)
        for j in range(count)
    ]
    routing = jnp.concatenate(
        [routes[...], numer[...], jnp.zeros((EXTRA - 3, tokens), jnp.int32)], axis=0
    )
    routing = routing.astype(F32).astype(BF16)
    for k in range(count):
        chosen = shares[k]
        for s in range(1, count):
            chosen = jnp.where(rank == s, shares[s ^ k], chosen)
        outs[k][:tokens, :] = chosen
        outs[k][tokens:, :] = jnp.zeros((EXTRA, chosen.shape[1]), BF16)
        outs[k][tokens:, :tokens] = routing
    for copy in copies:
        copy.wait()


def attend(lengths, matrix, queries, gain, routes, numer, kv_parts, carried, count):
    tokens = queries.shape[0]
    groups = kv_parts[0].shape[1] // (2 * HEAD_SIZE)
    per_group = QUERY_HEAD_COUNT // KEY_VALUE_HEADS
    split = pairwise(count)
    if split:
        out_shape = [
            jax.ShapeDtypeStruct((tokens + EXTRA, queries.shape[1] // count), BF16)
            for _ in range(count)
        ]
    else:
        out_shape = [jax.ShapeDtypeStruct(queries.shape, BF16)]
    length = tokens * count
    limit = min(40 << 20, (4 << 20) + 48 * per_group * tokens * length)
    out_shape = [
        jax.ShapeDtypeStruct((matrix.shape[0], gain.shape[2]), BF16),
        *[jax.ShapeDtypeStruct(array.shape, BF16) for array in (gain, *carried)],
    ] + out_shape
    return pl.pallas_call(
        functools.partial(
            attention_kernel, (tokens, groups, per_group, len(kv_parts), len(carried), split)
        ),
        out_shape=out_shape,
        in_specs=[SMEM, HBM] + [VMEM] * (4 + len(kv_parts)) + [ANY] * len(carried),
        out_specs=[VMEM] * len(out_shape),
        scratch_shapes=[pltpu.SemaphoreType.DMA((1 + len(carried),))],
        compiler_params=pltpu.CompilerParams(vmem_limit_bytes=limit),
        cost_estimate=pl.CostEstimate(
            flops=4 * tokens * length * queries.shape[1],
            bytes_accessed=4 * queries.size + 4 * length * kv_parts[0].shape[1],
            transcendentals=tokens * length * groups * per_group,
        ),
        name="attention",
    )(lengths, place(matrix, pltpu.HBM), queries, gain, routes, numer, *kv_parts, *carried)


def prepare_kernel(matrix, queries, keys, values, routes, numer, *refs):
    kv, rows, first_routes, weights = refs[:4]
    columns, sems = refs[4:-1], refs[-1]
    width = keys.shape[1]
    if columns:
        height, share = columns[0].shape
    pairs = [
        (keys, kv.at[:, :width]),
        (values, kv.at[:, width:]),
        (queries, rows),
        (routes, first_routes),
        (numer, weights),
    ]
    head, core = lax.axis_index("head"), lax.axis_index("dat")
    for m, out in enumerate(columns):
        lanes = pl.ds(pl.multiple_of(lax.bitwise_xor(head, m + 1) * share, share), share)
        if out.shape[0] == matrix.shape[0]:
            source = matrix.at[:, lanes]
        else:
            source = matrix.at[pl.ds(pl.multiple_of(core * height, height), height), lanes]
        pairs.insert(2, (source, out))
    copies = [pltpu.make_async_copy(*pair, sems.at[i]) for i, pair in enumerate(pairs)]
    for copy in copies:
        copy.start()
    for copy in copies:
        copy.wait()


def prepare(matrix, queries, keys, values, routes, numer, head_count, halves):
    rows, features = matrix.shape
    tokens = queries.shape[0]
    share = features // head_count
    out_shape = [
        jax.ShapeDtypeStruct((tokens, 2 * keys.shape[1]), BF16),
        jax.ShapeDtypeStruct(queries.shape, BF16),
        jax.ShapeDtypeStruct(routes.shape, jnp.int32),
        jax.ShapeDtypeStruct(numer.shape, jnp.int32),
    ] + [pltpu.VMEM((rows // halves, share), BF16)] * (head_count - 1)
    sources = [matrix, queries, keys, values, routes, numer]
    return pl.pallas_call(
        prepare_kernel,
        out_shape=out_shape,
        in_specs=[HBM] * len(sources),
        out_specs=[VMEM] * len(out_shape),
        scratch_shapes=[pltpu.SemaphoreType.DMA((4 + head_count,))],
        compiler_params=pltpu.CompilerParams(vmem_limit_bytes=8 << 20),
        cost_estimate=pl.CostEstimate(
            flops=0, bytes_accessed=4 * rows * features, transcendentals=0
        ),
        name="prepare",
    )(*[place(source, pltpu.HBM) for source in sources])


def project_kernel(parts, pieces, tokens, halves, *refs):
    rows = [sorted_back(refs[m * pieces : (m + 1) * pieces], ATTENDED_ORDER) for m in range(parts)]
    refs = refs[parts * pieces :]
    weights = [refs[:1]] + [refs[1 + m * halves : 1 + (m + 1) * halves] for m in range(parts - 1)]
    refs = refs[1 + (parts - 1) * halves :]
    outs = refs
    if tokens:
        route, outs = outs[0], outs[1:]
        route[...] = jnp.concatenate([ref[tokens : tokens + 8, :tokens] for ref in rows[0]], axis=1)
    total = None
    core = lax.axis_index("dat")
    for m in range(parts):
        stacked = jnp.concatenate([ref[: tokens or ref.shape[0]] for ref in rows[m]], axis=0)
        if len(weights[m]) == 1:
            factors = [stacked]
        else:
            half = stacked.shape[1] // 2
            low, high = stacked[:, :half], stacked[:, half:]
            factors = [jnp.where(core == 0, low, high), jnp.where(core == 0, high, low)]
        for factor, weight in zip(factors, weights[m]):
            product = jnp.dot(factor, weight[...], preferred_element_type=F32)
            total = product if total is None else total + product
    at = 0
    for i, out in enumerate(outs):
        out[...] = total[at : at + out.shape[0]].astype(out.dtype)
        at += out.shape[0]


def project(rows, weights, each):
    parts, pieces = len(rows), len(rows[0])
    depth, width = weights[0][0].shape
    flat_weights = [w for part in weights for w in part]
    heights = [each or p.shape[0] for p in rows[0]]
    tokens = sum(heights)
    out_shape = [
        jax.ShapeDtypeStruct((h, width), BF16 if each and i else F32)
        for i, h in enumerate(heights)
    ]
    if each:
        out_shape = [jax.ShapeDtypeStruct((8, tokens), BF16)] + out_shape
    flat = [p for part in rows for p in shuffled(part, ATTENDED_ORDER)]
    return pl.pallas_call(
        functools.partial(project_kernel, parts, pieces, each, len(weights[-1])),
        out_shape=out_shape,
        in_specs=[VMEM] * (len(flat) + len(flat_weights)),
        out_specs=[VMEM] * len(out_shape),
        compiler_params=pltpu.CompilerParams(vmem_limit_bytes=min(40 << 20, (4 << 20) + 16 * tokens * width)),
        cost_estimate=pl.CostEstimate(
            flops=2 * tokens * width * parts * depth,
            bytes_accessed=2 * parts * depth * width + 4 * tokens * width,
            transcendentals=0,
        ),
        name="projection",
    )(*flat, *flat_weights)


def fetch_kernel(chunk, gate_hbm, up_hbm, after, *refs):
    outs, done, sems = refs[:-2], refs[-2], refs[-1]
    per_expert = gate_hbm.shape[2] // chunk
    copies = []
    for step, out in enumerate(outs):
        at = pl.ds((step % per_expert) * chunk, chunk)
        for i, source in enumerate((gate_hbm, up_hbm)):
            copies.append(
                pltpu.make_async_copy(
                    source.at[step // per_expert, :, at], out.at[i], sems.at[step, i]
                )
            )
    for copy in copies:
        copy.start()
    done[...] = jnp.zeros_like(done)
    for copy in copies:
        copy.wait()


def fetch(expert_gate, expert_up, after, chunk, early, mark):
    features = expert_gate.shape[1]
    return pl.pallas_call(
        functools.partial(fetch_kernel, chunk),
        out_shape=[pltpu.VMEM((2, features, chunk), BF16)] * early
        + [
            jax.ShapeDtypeStruct((8, 128), F32),
        ],
        in_specs=[HBM, HBM, ANY],
        out_specs=[VMEM] * (early + 1),
        scratch_shapes=[pltpu.SemaphoreType.DMA((early, 2))],
        compiler_params=pltpu.CompilerParams(vmem_limit_bytes=1 << 20),
        cost_estimate=pl.CostEstimate(
            flops=0, bytes_accessed=8 * early * features * chunk, transcendentals=0
        ),
        name="fetch",
    )(place(expert_gate, pltpu.HBM), place(expert_up, pltpu.HBM), after)


def fetch_rows_kernel(chunk, early, gate_hbm, up_hbm, after, *refs):
    outs, sems = refs[:-1], refs[-1]
    width = outs[0].shape[1]
    per_expert = gate_hbm.shape[2] // chunk
    inner = pl.ds(pl.multiple_of(lax.axis_index("head") * width, width), width)
    copies = []
    for i, out in enumerate(outs):
        step = early + i
        at = pl.ds((step % per_expert) * chunk, chunk)
        for j, source in enumerate((gate_hbm, up_hbm)):
            copies.append(
                pltpu.make_async_copy(
                    source.at[step // per_expert, inner, at], out.at[j], sems.at[i, j]
                )
            )
    for copy in copies:
        copy.start()
    for copy in copies:
        copy.wait()


def fetch_rows(expert_gate, expert_up, after, chunk, early, width):
    experts, _, hidden_units = expert_gate.shape
    late = experts * (hidden_units // chunk) - early
    if not late:
        return []
    return pl.pallas_call(
        functools.partial(fetch_rows_kernel, chunk, early),
        out_shape=[pltpu.VMEM((2, width, chunk), BF16)] * late,
        in_specs=[HBM, HBM, ANY],
        out_specs=[VMEM] * late,
        scratch_shapes=[pltpu.SemaphoreType.DMA((late, 2))],
        compiler_params=pltpu.CompilerParams(vmem_limit_bytes=1 << 20),
        cost_estimate=pl.CostEstimate(
            flops=0, bytes_accessed=8 * late * width * chunk, transcendentals=0
        ),
        name="fetch_rows",
    )(place(expert_gate, pltpu.HBM), place(expert_up, pltpu.HBM), after)


def expert_kernel(shape, *refs):
    tokens, group, places, pieces, experts, slots, chunk, depth, early, ready, flips, first, last = shape
    parts = len(places)
    columns = [
        sorted_back(refs[m * pieces : (m + 1) * pieces], STREAM_ORDER) for m in range(parts)
    ]
    refs = refs[parts * pieces :]
    if first:
        routing, gain, refs = refs[0], refs[1], refs[2:]
    else:
        gain, picks, factors, squares_in, sums_in = refs[:5]
        refs = refs[5:]
    fetched, refs = refs[:early], refs[early:]
    fetched_rows, refs = refs[:ready], refs[ready:]
    gate_hbm, up_hbm, refs = refs[0], refs[1], refs[2:]
    if last:
        hidden, refs = refs[0], refs[1:]
    if first:
        picks, factors, refs = refs[0], refs[1], refs[2:]
    squares, sums, chosen, buffers, sems, out_sems = refs
    flip = lax.axis_index("seq") if flips else 0
    head = lax.axis_index("head")
    width = gain.shape[2]
    features = width * gain.shape[0]
    per_expert = gate_hbm.shape[2] // chunk
    steps = experts * per_expert
    size = group * tokens
    height = group * slots
    at_head = [lax.bitwise_xor(head, m) for m in places]
    inner = [pl.ds(pl.multiple_of(p * width, width), width) for p in at_head]

    def copies(step, slot):
        e, at = step // per_expert, pl.ds((step % per_expert) * chunk, chunk)
        return [
            pltpu.make_async_copy(
                source.at[e, inner[p], at], buffers.at[slot, i, p], sems.at[slot, i, p]
            )
            for p in range(parts)
            for i, source in enumerate((gate_hbm, up_hbm))
        ]

    for slot in range(depth):
        for copy in copies(early + slot, slot):
            copy.start()

    groups = picks.shape[0]
    if first:
        slot_row = lax.broadcasted_iota(jnp.int32, (height, size), 0)
        token_col = lax.broadcasted_iota(jnp.int32, (height, size), 1)
        row_block = lax.div(slot_row, slots)
        row_rank = slot_row - row_block * slots
        col_block = lax.bitwise_xor(lax.div(token_col, tokens), flip)
        same_block = row_block == col_block
        before_row = lax.broadcasted_iota(jnp.int32, (size, size), 0)
        before_col = lax.broadcasted_iota(jnp.int32, (size, size), 1)
        before = (
            (before_row < before_col)
            & (lax.div(before_row, tokens) == lax.div(before_col, tokens))
        ).astype(BF16)
        ranks = lax.broadcasted_iota(jnp.int32, (8, size), 0)
        for g in range(groups):
            route = routing[:, g * size : (g + 1) * size].astype(F32)
            first_route, second_route, weight = route[0:1], route[1:2], route[2:3] / 256.0
            gate_rows = []
            for e in range(experts):
                expert = (head * experts + e).astype(F32)
                gate_rows.append(
                    jnp.where(first_route == expert, weight, 0.0)
                    + jnp.where(second_route == expert, 1.0 - weight, 0.0)
                )
            marked = jnp.zeros((8, size), F32)
            for e in range(experts):
                marked = jnp.where(ranks == e, (gate_rows[e] > 0).astype(F32), marked)
            counted = jnp.dot(marked.astype(BF16), before, preferred_element_type=F32)
            for e in range(experts):
                hit = (
                    same_block
                    & (counted[e : e + 1].astype(jnp.int32) == row_rank)
                    & (gate_rows[e] > 0)
                )
                picks[g, e * height : (e + 1) * height, :] = hit.astype(BF16)
                factors[e, g * height : (g + 1) * height, :] = jnp.sum(
                    jnp.where(hit, gate_rows[e], 0.0), axis=1, keepdims=True
                )
    for g in range(groups):
        total = None
        for p in range(parts):
            if pieces > 1:
                tokens_in = jnp.concatenate([ref[...] for ref in columns[p]], axis=0)
            else:
                tokens_in = columns[p][0][g * size : (g + 1) * size]
            rows = jnp.dot(picks[g], tokens_in, preferred_element_type=F32)
            part = jnp.sum(rows * rows, axis=1, keepdims=True)
            total = part if total is None else total + part
            rows = (rows * gain[at_head[p]].astype(F32)).astype(BF16)
            for e in range(experts):
                chosen[p, e, g * height : (g + 1) * height, :] = rows[
                    e * height : (e + 1) * height
                ]
        for e in range(experts):
            at = slice(g * height, (g + 1) * height)
            here = total[e * height : (e + 1) * height]
            if not first:
                here = here + squares_in[e, at, :]
            squares[e, at, :] = here

    def compute(step, gate_of, up_of):
        e, begin = step // per_expert, (step % per_expert) * chunk
        at = slice(begin, begin + chunk)
        gate_part = up_part = None
        for p in range(parts):
            rows = chosen[p, e]
            a = jnp.dot(rows, gate_of(p), preferred_element_type=F32)
            b = jnp.dot(rows, up_of(p), preferred_element_type=F32)
            gate_part = a if gate_part is None else gate_part + a
            up_part = b if up_part is None else up_part + b
        if not first:
            gate_part = gate_part + sums_in[0, e, :, at]
            up_part = up_part + sums_in[1, e, :, at]
        if not last:
            sums[0, e, :, at] = gate_part
            sums[1, e, :, at] = up_part
            return
        scale = lax.rsqrt(squares[e] / features + EPS)
        gate_part, up_part = gate_part * scale, up_part * scale
        result = factors[e] * (gate_part / (1.0 + jnp.exp(-gate_part)) * up_part)
        sums[e, :, at] = result.astype(BF16)
        store(step).start()

    def store(step):
        e, at = step // per_expert, pl.ds((step % per_expert) * chunk, chunk)
        return pltpu.make_async_copy(sums.at[e, :, at], hidden.at[e, :, at], out_sems.at[step])

    late = list(range(early + ready, steps))
    soon = len(late) - depth if late else 0
    order = [*range(early // 2), *late[:soon], *range(early // 2, early + ready), *late[soon:]]
    for step in order:
        if step < early:
            ref = fetched[step]
            compute(step, lambda p: ref[0, inner[p], :], lambda p: ref[1, inner[p], :])
            continue
        if step < early + ready:
            ref = fetched_rows[step - early]
            compute(step, lambda p: ref[0], lambda p: ref[1])
            continue
        slot = (step - early) % depth
        for copy in copies(step, slot):
            copy.wait()
        compute(
            step, lambda p: buffers[slot, 0, p], lambda p: buffers[slot, 1, p]
        )
        if step + depth < steps:
            for copy in copies(step + depth, slot):
                copy.start()
    if last:
        for step in range(steps):
            store(step).wait()


def run_experts(
    columns, places, gain, fetched, fetched_rows, matrices, tokens, count, carried, last
):
    first = len(carried) == 1
    parts, pieces = len(columns), len(columns[0])
    experts, features, hidden_units = matrices[0].shape
    width = gain.shape[2]
    early, chunk = len(fetched), fetched[0].shape[2]
    ready = len(fetched_rows)
    steps = experts * (hidden_units // chunk)
    depth = min(4, steps - early - ready)
    group = min(4, count)
    slots = MOST * count
    shape = (tokens, group, places, pieces, experts, MOST, chunk, depth, early, ready, pairwise(count), first, last)
    flat = [p for part in columns for p in shuffled(part, STREAM_ORDER)]
    routing, carried = (carried, []) if first else ([], carried)
    kept = [
        jax.ShapeDtypeStruct((count // group, experts * group * MOST, group * tokens), BF16),
        jax.ShapeDtypeStruct((experts, slots, 1), F32),
    ]
    passed = [
        jax.ShapeDtypeStruct((experts, slots, 1), F32),
        jax.ShapeDtypeStruct((2, experts, slots, hidden_units), F32),
    ]
    out_shape = [jax.ShapeDtypeStruct((experts, slots, hidden_units), BF16)] if last else []
    scratch = []
    for wanted, shapes in ((first, kept), (True, passed)):
        if wanted and last:
            scratch += [pltpu.VMEM(a.shape, a.dtype) for a in shapes]
        elif wanted:
            out_shape += shapes
    if last:
        scratch[-1] = pltpu.VMEM((experts, slots, hidden_units), BF16)
    small = count <= 4
    limit = (6 << 20) if small and not last else (10 << 20) if small else 44 << 20
    return pl.pallas_call(
        functools.partial(expert_kernel, shape),
        out_shape=out_shape,
        in_specs=[VMEM] * (len(flat) + len(routing) + 1 + len(carried) + early + ready)
        + [HBM, HBM],
        out_specs=[ANY] * last + [VMEM] * (len(out_shape) - last),
        scratch_shapes=scratch
        + [
            pltpu.VMEM((parts, experts, slots, width), BF16),
            pltpu.VMEM((max(depth, 1), 2, parts, width if depth else 16, chunk), BF16),
            pltpu.SemaphoreType.DMA((max(depth, 1), 2, parts)),
            pltpu.SemaphoreType.DMA((steps,)),
        ],
        compiler_params=pltpu.CompilerParams(vmem_limit_bytes=limit),
        cost_estimate=pl.CostEstimate(
            flops=4 * experts * slots * width * parts * hidden_units,
            bytes_accessed=2 * matrices[0].size,
            transcendentals=experts * slots * hidden_units,
        ),
        name="experts",
    )(
        *flat,
        *routing,
        gain,
        *carried,
        *[place(part, pltpu.VMEM) for part in (*fetched, *fetched_rows)],
        *[place(matrix, pltpu.HBM) for matrix in matrices],
    )


def local(
    queries,
    keys,
    values,
    residual_in,
    out_proj,
    norm_gain,
    expert_gate,
    expert_up,
    routes,
    gate_numer,
    sequence_lengths,
):
    tokens = queries.shape[1]
    count = lax.axis_size("seq")
    head_count = lax.axis_size("head")
    split = pairwise(count)
    share = residual_in.shape[2]
    features = out_proj.shape[2]
    heads, part, _ = out_proj.shape

    matrix = out_proj.reshape(heads * part, features)
    halves = 2 if lax.axis_size("dat") == 2 and matrix.shape[0] % 32 == 0 else 1
    own_kv, rows, own_routes, numer, *weights = prepare(
        matrix, queries[0], keys[0], values[0], routes[0].T, gate_numer, head_count, halves
    )

    weights = [swap(weights[m - 1], "head", m) for m in range(1, head_count)]

    kv_parts = spread(own_kv, "seq", upward=True)
    gain = norm_gain.reshape(head_count, 1, share)

    own_weights, gain, *attended = attend(
        sequence_lengths,
        matrix,
        rows,
        gain,
        own_routes,
        numer,
        kv_parts,
        weights if halves == 2 else [],
        count,
    )
    if halves == 2:
        carried, attended = attended[: head_count - 1], attended[head_count - 1 :]
        weights = [[got, swap(again, "dat", 1)] for got, again in zip(weights, carried)]
    else:
        weights = [[got] for got in weights]
    weights = [[own_weights]] + weights
    if split:
        attended = swaps(attended, "seq")
    else:
        shares = attended[0].reshape(tokens, heads, count, part).transpose(2, 0, 1, 3)
        shares = shares.reshape(count * tokens, heads * part)
        attended = [lax.all_to_all(shares, "seq", 0, 0, tiled=True)]
        routing = jnp.concatenate(
            [own_routes, numer, jnp.zeros((5, tokens), jnp.int32)], axis=0
        )
        routing = lax.all_gather(routing, "seq", axis=1, tiled=True)
    rows = [attended] + [
        [swap(piece, "head", m) for piece in attended] for m in range(1, head_count)
    ]
    sums = project(rows, weights, tokens if split else 0)
    if split:
        routing, *sums = sums
    chunk = min(256, expert_gate.shape[2])
    early = max(1, expert_gate.shape[0] * (expert_gate.shape[2] // chunk) * 11 // 16)
    *fetched, done = fetch(expert_gate, expert_up, sums[-1], chunk, early, share)
    if split:
        received = swaps(sums, "seq")[1:]
        mixed = sums[0]
        for part_sum in received:
            mixed = mixed + part_sum.astype(F32)
    else:
        mixed = lax.psum_scatter(sums[0], "seq", scatter_dimension=0, tiled=True)

    stream = (residual_in[0].astype(F32) + mixed + done[:1, :1]).astype(BF16)
    own_columns = spread(stream, "seq")
    columns = [own_columns] + [
        [swap(piece, "head", m) for piece in own_columns] for m in range(1, head_count)
    ]
    passes = [[0], list(range(1, head_count))] if head_count > 1 else [[0]]
    fetched_rows = fetch_rows(expert_gate, expert_up, stream, chunk, early, share)
    carried = [routing]
    for i, places in enumerate(passes):
        carried = run_experts(
            [columns[m] for m in places],
            tuple(places),
            gain,
            fetched,
            [] if i else fetched_rows,
            (expert_gate, expert_up),
            tokens,
            count,
            carried,
            i == len(passes) - 1,
        )
    hidden = carried[0]
    return (stream[None], hidden[:, None])


def solution(mesh):
    in_specs = (
        P(("grp", "dat"), "seq", "head"),
        P(("grp", "dat"), "seq", "head"),
        P(("grp", "dat"), "seq", "head"),
        P(("grp", "dat"), "seq", "head"),
        P("head", "seq", None),
        P(),
        P("head", None, "seq"),
        P("head", None, "seq"),
        P(("grp", "dat"), "seq", None),
        P(("grp", "dat"), "seq"),
        P(("grp", "dat")),
    )
    out_specs = (P(("grp", "dat"), "seq", "head"), P("head", ("grp", "dat"), None, "seq"))
    return jax.shard_map(local, mesh=mesh, in_specs=in_specs, out_specs=out_specs, check_vma=False)
```

```python
import functools
import math

import jax
import jax.numpy as jnp
from jax import lax
from jax.experimental import pallas as pl
from jax.experimental.pallas import tpu as pltpu
from jax.sharding import PartitionSpec as P

HEAD_SIZE = 128
QUERY_HEAD_COUNT = 24
KEY_VALUE_HEADS = 4
MOST = 40
EXTRA = 16
ATTENDED_ORDER = (0, 3, 2, 1)
STREAM_ORDER = (0, 3, 1, 2)
EPS = 1e-05
NEG = -1e30
F32 = jnp.float32
BF16 = jnp.bfloat16

VMEM = pl.BlockSpec(memory_space=pltpu.VMEM)
SMEM = pl.BlockSpec(memory_space=pltpu.SMEM)
ANY = pl.BlockSpec(memory_space=pl.ANY)
place = pltpu.with_memory_space_constraint
HBM = pl.BlockSpec(memory_space=pltpu.HBM)


def pairwise(count):
    return count in (1, 2, 4)


def swap(array, axis, step, upward=False):
    count = lax.axis_size(axis)
    pairs = [(i, i ^ step) for i in range(count) if not upward or i < i ^ step]
    return lax.ppermute(array, axis, pairs)


def steps_of(count):
    return [k for k in (2, 3, 1) if k < count]


def shuffled(pieces, order):
    return [pieces[k] for k in order] if len(pieces) == len(order) else list(pieces)


def sorted_back(pieces, order):
    return [pieces[order.index(k)] for k in range(4)] if len(pieces) == len(order) else list(pieces)


def swaps(arrays, axis, upward=False):
    got = {k: swap(arrays[k], axis, k, upward) for k in steps_of(len(arrays))}
    return [arrays[0]] + [got[k] for k in range(1, len(arrays))]


def spread(array, axis, upward=False):
    count = lax.axis_size(axis)
    if pairwise(count):
        return swaps([array] * count, axis, upward)
    return [lax.all_gather(array, axis, axis=0, tiled=True)]


def attention_kernel(shape, lengths, matrix, queries, gain_in, routes, numer, *refs):
    tokens, groups, per_group, pieces, split = shape
    kv_refs, refs = refs[:pieces], refs[pieces:]
    own, gain_out, outs, sem = refs[0], refs[1], refs[2:-1], refs[-1]
    rank = lax.axis_index("seq")
    share = own.shape[1]
    lanes = pl.ds(pl.multiple_of(lax.axis_index("head") * share, share), share)
    copy = pltpu.make_async_copy(matrix.at[:, lanes], own, sem)
    copy.start()
    gain_out[...] = gain_in[...]
    flip, valid_len = rank if split else 0, lengths[0]
    width = groups * HEAD_SIZE
    key_parts = [ref[:, :width] for ref in kv_refs]
    value_parts = [ref[:, width:] for ref in kv_refs]
    all_keys = jnp.concatenate(key_parts, axis=0)
    all_values = jnp.concatenate(value_parts, axis=0)
    length = all_keys.shape[0]
    column = lax.broadcasted_iota(jnp.int32, (tokens, length), 1)
    block = lax.div(column, tokens)
    key_pos = lax.bitwise_xor(block, flip) * tokens + (column - block * tokens)
    query_pos = rank * tokens + lax.broadcasted_iota(jnp.int32, (tokens, length), 0)
    allowed = ((key_pos <= query_pos) & (key_pos < valid_len)).astype(F32)
    allowed = jnp.concatenate([allowed] * per_group, axis=0) > 0
    scale = 1.0 / math.sqrt(HEAD_SIZE)
    attended = []
    for g in range(groups):
        heads = [g * per_group + a for a in range(per_group)]
        rows = jnp.concatenate(
            [queries[:, h * HEAD_SIZE : (h + 1) * HEAD_SIZE] for h in heads], axis=0
        )
        lanes = slice(g * HEAD_SIZE, (g + 1) * HEAD_SIZE)
        scores = (
            lax.dot_general(
                rows, all_keys[:, lanes], (((1,), (1,)), ((), ())), preferred_element_type=F32
            )
            * scale
        )
        scores = jnp.where(allowed, scores, NEG)
        top = jnp.max(scores, axis=-1, keepdims=True)
        weights = jnp.where(allowed, jnp.exp(scores - top), 0.0)
        denom = jnp.sum(weights, axis=-1, keepdims=True)
        mixed = jnp.dot(weights.astype(BF16), all_values[:, lanes], preferred_element_type=F32)
        mixed = mixed / denom
        attended += [mixed[a * tokens : (a + 1) * tokens] for a in range(per_group)]
    if not split:
        outs[0][...] = jnp.concatenate(attended, axis=1).astype(BF16)
        copy.wait()
        return
    count = len(outs)
    part = HEAD_SIZE // count
    shares = [
        jnp.concatenate([o[:, j * part : (j + 1) * part] for o in attended], axis=1).astype(BF16)
        for j in range(count)
    ]
    routing = jnp.concatenate(
        [routes[...], numer[...], jnp.zeros((EXTRA - 3, tokens), jnp.int32)], axis=0
    )
    routing = routing.astype(F32).astype(BF16)
    for k in range(count):
        chosen = shares[k]
        for s in range(1, count):
            chosen = jnp.where(rank == s, shares[s ^ k], chosen)
        outs[k][:tokens, :] = chosen
        outs[k][tokens:, :] = jnp.zeros((EXTRA, chosen.shape[1]), BF16)
        outs[k][tokens:, :tokens] = routing
    copy.wait()


def attend(lengths, matrix, queries, gain, routes, numer, kv_parts, count):
    tokens = queries.shape[0]
    groups = kv_parts[0].shape[1] // (2 * HEAD_SIZE)
    per_group = QUERY_HEAD_COUNT // KEY_VALUE_HEADS
    split = pairwise(count)
    if split:
        out_shape = [
            jax.ShapeDtypeStruct((tokens + EXTRA, queries.shape[1] // count), BF16)
            for _ in range(count)
        ]
    else:
        out_shape = [jax.ShapeDtypeStruct(queries.shape, BF16)]
    length = tokens * count
    limit = min(40 << 20, (4 << 20) + 48 * per_group * tokens * length)
    out_shape = [
        jax.ShapeDtypeStruct((matrix.shape[0], gain.shape[2]), BF16),
        jax.ShapeDtypeStruct(gain.shape, BF16),
    ] + out_shape
    return pl.pallas_call(
        functools.partial(
            attention_kernel, (tokens, groups, per_group, len(kv_parts), split)
        ),
        out_shape=out_shape,
        in_specs=[SMEM, HBM] + [VMEM] * (4 + len(kv_parts)),
        out_specs=[VMEM] * len(out_shape),
        scratch_shapes=[pltpu.SemaphoreType.DMA],
        compiler_params=pltpu.CompilerParams(vmem_limit_bytes=limit),
        cost_estimate=pl.CostEstimate(
            flops=4 * tokens * length * queries.shape[1],
            bytes_accessed=4 * queries.size + 4 * length * kv_parts[0].shape[1],
            transcendentals=tokens * length * groups * per_group,
        ),
        name="attention",
    )(lengths, place(matrix, pltpu.HBM), queries, gain, routes, numer, *kv_parts)


def prepare_kernel(matrix, queries, keys, values, routes, numer, *refs):
    kv, rows, first_routes, weights = refs[:4]
    columns, sems = refs[4:-1], refs[-1]
    width = keys.shape[1]
    if columns:
        height, share = columns[0].shape
    pairs = [
        (keys, kv.at[:, :width]),
        (values, kv.at[:, width:]),
        (queries, rows),
        (routes, first_routes),
        (numer, weights),
    ]
    head, core = lax.axis_index("head"), lax.axis_index("dat")
    for m, out in enumerate(columns):
        lanes = pl.ds(pl.multiple_of(lax.bitwise_xor(head, m + 1) * share, share), share)
        if out.shape[0] == matrix.shape[0]:
            source = matrix.at[:, lanes]
        else:
            source = matrix.at[pl.ds(pl.multiple_of(core * height, height), height), lanes]
        pairs.insert(2, (source, out))
    copies = [pltpu.make_async_copy(*pair, sems.at[i]) for i, pair in enumerate(pairs)]
    for copy in copies:
        copy.start()
    for copy in copies:
        copy.wait()


def prepare(matrix, queries, keys, values, routes, numer, head_count, halves):
    rows, features = matrix.shape
    tokens = queries.shape[0]
    share = features // head_count
    out_shape = [
        jax.ShapeDtypeStruct((tokens, 2 * keys.shape[1]), BF16),
        jax.ShapeDtypeStruct(queries.shape, BF16),
        jax.ShapeDtypeStruct(routes.shape, jnp.int32),
        jax.ShapeDtypeStruct(numer.shape, jnp.int32),
    ] + [pltpu.VMEM((rows // halves, share), BF16)] * (head_count - 1)
    sources = [matrix, queries, keys, values, routes, numer]
    return pl.pallas_call(
        prepare_kernel,
        out_shape=out_shape,
        in_specs=[HBM] * len(sources),
        out_specs=[VMEM] * len(out_shape),
        scratch_shapes=[pltpu.SemaphoreType.DMA((4 + head_count,))],
        compiler_params=pltpu.CompilerParams(vmem_limit_bytes=8 << 20),
        cost_estimate=pl.CostEstimate(
            flops=0, bytes_accessed=4 * rows * features, transcendentals=0
        ),
        name="prepare",
    )(*[place(source, pltpu.HBM) for source in sources])


def pack_kernel(tokens, pieces, *refs):
    parts, refs = sorted_back(refs[:pieces], ATTENDED_ORDER), refs[pieces:]
    carried = (len(refs) - 3) // 2
    carried_in, packed, route, refs = refs[:carried], refs[carried], refs[carried + 1], refs[carried + 2 :]
    copies = [
        pltpu.make_async_copy(source, out, refs[-1].at[i])
        for i, (source, out) in enumerate(zip(carried_in, refs[:-1]))
    ]
    for copy in copies:
        copy.start()
    for k, ref in enumerate(parts):
        at = slice(k * tokens, (k + 1) * tokens)
        packed[at, :] = ref[:tokens, :]
        route[:, at] = ref[tokens : tokens + 8, :tokens]
    for copy in copies:
        copy.wait()


def pack(parts, tokens, carried):
    width = parts[0].shape[1]
    rows = tokens * len(parts)
    out_shape = [
        jax.ShapeDtypeStruct((rows, width), BF16),
        jax.ShapeDtypeStruct((8, rows), BF16),
        *[jax.ShapeDtypeStruct(array.shape, array.dtype) for array in carried],
    ]
    return pl.pallas_call(
        functools.partial(pack_kernel, tokens, len(parts)),
        out_shape=out_shape,
        in_specs=[VMEM] * len(parts) + [ANY] * len(carried),
        out_specs=[VMEM] * len(out_shape),
        scratch_shapes=[pltpu.SemaphoreType.DMA((max(1, len(carried)),))],
        compiler_params=pltpu.CompilerParams(vmem_limit_bytes=6 << 20),
        name="pack",
    )(*shuffled(parts, ATTENDED_ORDER), *carried)


def project_kernel(parts, halves, *refs):
    rows, refs = refs[:parts], refs[parts:]
    weights = [refs[:1]] + [refs[1 + m * halves : 1 + (m + 1) * halves] for m in range(parts - 1)]
    outs = refs[1 + (parts - 1) * halves :]
    core = lax.axis_index("dat")
    total = None
    for m in range(parts):
        factors = [rows[m][...]]
        if len(weights[m]) > 1:
            half = rows[m].shape[1] // 2
            low, high = factors[0][:, :half], factors[0][:, half:]
            factors = [jnp.where(core == 0, low, high), jnp.where(core == 0, high, low)]
        for factor, weight in zip(factors, weights[m]):
            product = jnp.dot(factor, weight[...], preferred_element_type=F32)
            total = product if total is None else total + product
    at = 0
    for out in outs:
        out[...] = total[at : at + out.shape[0]].astype(out.dtype)
        at += out.shape[0]


def project(rows, weights, pieces):
    parts, (tokens, depth), width = len(rows), rows[0].shape, weights[0][0].shape[1]
    flat_weights = [w for part in weights for w in part]
    return pl.pallas_call(
        functools.partial(project_kernel, parts, len(weights[-1])),
        out_shape=[
            jax.ShapeDtypeStruct((tokens // pieces, width), BF16 if i else F32)
            for i in range(pieces)
        ],
        in_specs=[VMEM] * (parts + len(flat_weights)),
        out_specs=[VMEM] * pieces,
        compiler_params=pltpu.CompilerParams(
            vmem_limit_bytes=min(40 << 20, (4 << 20) + 16 * tokens * width)
        ),
        cost_estimate=pl.CostEstimate(
            flops=2 * tokens * width * parts * depth,
            bytes_accessed=2 * parts * depth * width + 4 * tokens * width,
            transcendentals=0,
        ),
        name="projection",
    )(*rows, *flat_weights)


def fetch_kernel(chunk, gate_hbm, up_hbm, kept, *refs):
    outs, done, sems = refs[:-2], refs[-2], refs[-1]
    per_expert = gate_hbm.shape[2] // chunk
    copies = []
    for step, out in enumerate(outs):
        at = pl.ds((step % per_expert) * chunk, chunk)
        for i, source in enumerate((gate_hbm, up_hbm)):
            copies.append(
                pltpu.make_async_copy(
                    source.at[step // per_expert, :, at], out.at[i], sems.at[step, i]
                )
            )
    for copy in copies:
        copy.start()
    done[...] = kept[...]
    for copy in copies:
        copy.wait()


def fetch(expert_gate, expert_up, kept, chunk, early):
    features = expert_gate.shape[1]
    return pl.pallas_call(
        functools.partial(fetch_kernel, chunk),
        out_shape=[pltpu.VMEM((2, features, chunk), BF16)] * early
        + [
            jax.ShapeDtypeStruct(kept.shape, F32),
        ],
        in_specs=[HBM, HBM, VMEM],
        out_specs=[VMEM] * (early + 1),
        scratch_shapes=[pltpu.SemaphoreType.DMA((early, 2))],
        compiler_params=pltpu.CompilerParams(vmem_limit_bytes=4 << 20 if kept.size < 1 << 20 else 40 << 20),
        cost_estimate=pl.CostEstimate(
            flops=0, bytes_accessed=8 * early * features * chunk, transcendentals=0
        ),
        name="fetch",
    )(place(expert_gate, pltpu.HBM), place(expert_up, pltpu.HBM), kept)


def fetch_rows_kernel(chunk, early, gate_hbm, up_hbm, after, *refs):
    outs, sems = refs[:-1], refs[-1]
    width = outs[0].shape[1]
    per_expert = gate_hbm.shape[2] // chunk
    inner = pl.ds(pl.multiple_of(lax.axis_index("head") * width, width), width)
    copies = []
    for i, out in enumerate(outs):
        step = early + i
        at = pl.ds((step % per_expert) * chunk, chunk)
        for j, source in enumerate((gate_hbm, up_hbm)):
            copies.append(
                pltpu.make_async_copy(
                    source.at[step // per_expert, inner, at], out.at[j], sems.at[i, j]
                )
            )
    for copy in copies:
        copy.start()
    for copy in copies:
        copy.wait()


def fetch_rows(expert_gate, expert_up, after, chunk, early, width):
    experts, _, hidden_units = expert_gate.shape
    late = experts * (hidden_units // chunk) - early
    if not late:
        return []
    return pl.pallas_call(
        functools.partial(fetch_rows_kernel, chunk, early),
        out_shape=[pltpu.VMEM((2, width, chunk), BF16)] * late,
        in_specs=[HBM, HBM, ANY],
        out_specs=[VMEM] * late,
        scratch_shapes=[pltpu.SemaphoreType.DMA((late, 2))],
        compiler_params=pltpu.CompilerParams(vmem_limit_bytes=1 << 20),
        cost_estimate=pl.CostEstimate(
            flops=0, bytes_accessed=8 * late * width * chunk, transcendentals=0
        ),
        name="fetch_rows",
    )(place(expert_gate, pltpu.HBM), place(expert_up, pltpu.HBM), after)


def expert_kernel(shape, *refs):
    tokens, group, places, pieces, experts, slots, chunk, depth, early, ready, flips, first, last = shape
    parts = len(places)
    columns = [
        sorted_back(refs[m * pieces : (m + 1) * pieces], STREAM_ORDER) for m in range(parts)
    ]
    refs = refs[parts * pieces :]
    if first:
        routing, gain, refs = refs[0], refs[1], refs[2:]
    else:
        gain, picks, factors, squares_in, sums_in = refs[:5]
        refs = refs[5:]
    fetched, refs = refs[:early], refs[early:]
    fetched_rows, refs = refs[:ready], refs[ready:]
    gate_hbm, up_hbm, refs = refs[0], refs[1], refs[2:]
    if last:
        hidden, refs = refs[0], refs[1:]
    if first:
        picks, factors, refs = refs[0], refs[1], refs[2:]
    squares, sums, chosen, buffers, sems, out_sems = refs
    flip = lax.axis_index("seq") if flips else 0
    head = lax.axis_index("head")
    width = gain.shape[2]
    features = width * gain.shape[0]
    per_expert = gate_hbm.shape[2] // chunk
    steps = experts * per_expert
    size = group * tokens
    height = group * slots
    at_head = [lax.bitwise_xor(head, m) for m in places]
    inner = [pl.ds(pl.multiple_of(p * width, width), width) for p in at_head]

    def copies(step, slot):
        e, at = step // per_expert, pl.ds((step % per_expert) * chunk, chunk)
        return [
            pltpu.make_async_copy(
                source.at[e, inner[p], at], buffers.at[slot, i, p], sems.at[slot, i, p]
            )
            for p in range(parts)
            for i, source in enumerate((gate_hbm, up_hbm))
        ]

    for slot in range(depth):
        for copy in copies(early + slot, slot):
            copy.start()

    groups = picks.shape[0]
    if first:
        slot_row = lax.broadcasted_iota(jnp.int32, (height, size), 0)
        token_col = lax.broadcasted_iota(jnp.int32, (height, size), 1)
        row_block = lax.div(slot_row, slots)
        row_rank = slot_row - row_block * slots
        col_block = lax.bitwise_xor(lax.div(token_col, tokens), flip)
        same_block = row_block == col_block
        before_row = lax.broadcasted_iota(jnp.int32, (size, size), 0)
        before_col = lax.broadcasted_iota(jnp.int32, (size, size), 1)
        before = (
            (before_row < before_col)
            & (lax.div(before_row, tokens) == lax.div(before_col, tokens))
        ).astype(BF16)
        ranks = lax.broadcasted_iota(jnp.int32, (8, size), 0)
        for g in range(groups):
            route = routing[:, g * size : (g + 1) * size].astype(F32)
            first_route, second_route, weight = route[0:1], route[1:2], route[2:3] / 256.0
            gate_rows = []
            for e in range(experts):
                expert = (head * experts + e).astype(F32)
                gate_rows.append(
                    jnp.where(first_route == expert, weight, 0.0)
                    + jnp.where(second_route == expert, 1.0 - weight, 0.0)
                )
            marked = jnp.zeros((8, size), F32)
            for e in range(experts):
                marked = jnp.where(ranks == e, (gate_rows[e] > 0).astype(F32), marked)
            counted = jnp.dot(marked.astype(BF16), before, preferred_element_type=F32)
            for e in range(experts):
                hit = (
                    same_block
                    & (counted[e : e + 1].astype(jnp.int32) == row_rank)
                    & (gate_rows[e] > 0)
                )
                picks[g, e * height : (e + 1) * height, :] = hit.astype(BF16)
                factors[e, g * height : (g + 1) * height, :] = jnp.sum(
                    jnp.where(hit, gate_rows[e], 0.0), axis=1, keepdims=True
                )
    for g in range(groups):
        total = None
        for p in range(parts):
            if pieces > 1:
                tokens_in = jnp.concatenate([ref[...] for ref in columns[p]], axis=0)
            else:
                tokens_in = columns[p][0][g * size : (g + 1) * size]
            rows = jnp.dot(picks[g], tokens_in, preferred_element_type=F32)
            part = jnp.sum(rows * rows, axis=1, keepdims=True)
            total = part if total is None else total + part
            rows = (rows * gain[at_head[p]].astype(F32)).astype(BF16)
            for e in range(experts):
                chosen[p, e, g * height : (g + 1) * height, :] = rows[
                    e * height : (e + 1) * height
                ]
        for e in range(experts):
            at = slice(g * height, (g + 1) * height)
            here = total[e * height : (e + 1) * height]
            if not first:
                here = here + squares_in[e, at, :]
            squares[e, at, :] = here

    def compute(step, gate_of, up_of):
        e, begin = step // per_expert, (step % per_expert) * chunk
        at = slice(begin, begin + chunk)
        gate_part = up_part = None
        for p in range(parts):
            rows = chosen[p, e]
            a = jnp.dot(rows, gate_of(p), preferred_element_type=F32)
            b = jnp.dot(rows, up_of(p), preferred_element_type=F32)
            gate_part = a if gate_part is None else gate_part + a
            up_part = b if up_part is None else up_part + b
        if not first:
            gate_part = gate_part + sums_in[0, e, :, at].astype(F32)
            up_part = up_part + sums_in[1, e, :, at].astype(F32)
        if not last:
            sums[0, e, :, at] = gate_part.astype(BF16)
            sums[1, e, :, at] = up_part.astype(BF16)
            return
        scale = lax.rsqrt(squares[e] / features + EPS)
        gate_part, up_part = gate_part * scale, up_part * scale
        result = factors[e] * (gate_part / (1.0 + jnp.exp(-gate_part)) * up_part)
        sums[e, :, at] = result.astype(BF16)
        store(step).start()

    def store(step):
        e, at = step // per_expert, pl.ds((step % per_expert) * chunk, chunk)
        return pltpu.make_async_copy(sums.at[e, :, at], hidden.at[e, :, at], out_sems.at[step])

    late = list(range(early + ready, steps))
    soon = len(late) - depth if late else 0
    order = [*range(early // 2), *late[:soon], *range(early // 2, early + ready), *late[soon:]]
    for step in order:
        if step < early:
            ref = fetched[step]
            compute(step, lambda p: ref[0, inner[p], :], lambda p: ref[1, inner[p], :])
            continue
        if step < early + ready:
            ref = fetched_rows[step - early]
            compute(step, lambda p: ref[0], lambda p: ref[1])
            continue
        slot = (step - early) % depth
        for copy in copies(step, slot):
            copy.wait()
        compute(
            step, lambda p: buffers[slot, 0, p], lambda p: buffers[slot, 1, p]
        )
        if step + depth < steps:
            for copy in copies(step + depth, slot):
                copy.start()
    if last:
        for step in range(steps):
            store(step).wait()


def run_experts(
    columns, places, gain, fetched, fetched_rows, matrices, tokens, count, carried, last
):
    first = len(carried) == 1
    parts, pieces = len(columns), len(columns[0])
    experts, features, hidden_units = matrices[0].shape
    width = gain.shape[2]
    early, chunk = len(fetched), fetched[0].shape[2]
    ready = len(fetched_rows)
    steps = experts * (hidden_units // chunk)
    depth = min(3, steps - early - ready)
    group = min(4, count)
    slots = MOST * count
    shape = (tokens, group, places, pieces, experts, MOST, chunk, depth, early, ready, pairwise(count), first, last)
    flat = [p for part in columns for p in shuffled(part, STREAM_ORDER)]
    routing, carried = (carried, []) if first else ([], carried)
    kept = [
        jax.ShapeDtypeStruct((count // group, experts * group * MOST, group * tokens), BF16),
        jax.ShapeDtypeStruct((experts, slots, 1), F32),
    ]
    passed = [
        jax.ShapeDtypeStruct((experts, slots, 1), F32),
        jax.ShapeDtypeStruct((2, experts, slots, hidden_units), BF16),
    ]
    out_shape = [jax.ShapeDtypeStruct((experts, slots, hidden_units), BF16)] if last else []
    scratch = []
    for wanted, shapes in ((first, kept), (True, passed)):
        if wanted and last:
            scratch += [pltpu.VMEM(a.shape, a.dtype) for a in shapes]
        elif wanted:
            out_shape += shapes
    if last:
        scratch[-1] = pltpu.VMEM((experts, slots, hidden_units), BF16)
    small = count <= 4
    limit = (6 << 20) if small and not last else (9 << 20) if small else 44 << 20
    return pl.pallas_call(
        functools.partial(expert_kernel, shape),
        out_shape=out_shape,
        in_specs=[VMEM] * (len(flat) + len(routing) + 1 + len(carried) + early + ready)
        + [HBM, HBM],
        out_specs=[ANY] * last + [VMEM] * (len(out_shape) - last),
        scratch_shapes=scratch
        + [
            pltpu.VMEM((parts, experts, slots, width), BF16),
            pltpu.VMEM((max(depth, 1), 2, parts, width if depth else 16, chunk), BF16),
            pltpu.SemaphoreType.DMA((max(depth, 1), 2, parts)),
            pltpu.SemaphoreType.DMA((steps,)),
        ],
        compiler_params=pltpu.CompilerParams(vmem_limit_bytes=limit),
        cost_estimate=pl.CostEstimate(
            flops=4 * experts * slots * width * parts * hidden_units,
            bytes_accessed=2 * matrices[0].size,
            transcendentals=experts * slots * hidden_units,
        ),
        name="experts",
    )(
        *flat,
        *routing,
        gain,
        *carried,
        *[place(part, pltpu.VMEM) for part in (*fetched, *fetched_rows)],
        *[place(matrix, pltpu.HBM) for matrix in matrices],
    )


def local(
    queries,
    keys,
    values,
    residual_in,
    out_proj,
    norm_gain,
    expert_gate,
    expert_up,
    routes,
    gate_numer,
    sequence_lengths,
):
    tokens = queries.shape[1]
    count = lax.axis_size("seq")
    head_count = lax.axis_size("head")
    split = pairwise(count)
    share = residual_in.shape[2]
    features = out_proj.shape[2]
    heads, part, _ = out_proj.shape

    matrix = out_proj.reshape(heads * part, features)
    halves = 2 if lax.axis_size("dat") == 2 and matrix.shape[0] % 32 == 0 else 1
    own_kv, rows, own_routes, numer, *weights = prepare(
        matrix, queries[0], keys[0], values[0], routes[0].T, gate_numer, head_count, halves
    )

    weights = [swap(weights[m - 1], "head", m) for m in range(1, head_count)]

    kv_parts = spread(own_kv, "seq")
    gain = norm_gain.reshape(head_count, 1, share)

    own_weights, gain, *attended = attend(
        sequence_lengths, matrix, rows, gain, own_routes, numer, kv_parts, count
    )
    if split:
        attended = swaps(attended, "seq")
        mine, routing, *carried = pack(attended, tokens, weights if halves == 2 else [])
    else:
        shares = attended[0].reshape(tokens, heads, count, part).transpose(2, 0, 1, 3)
        shares = shares.reshape(count * tokens, heads * part)
        mine = lax.all_to_all(shares, "seq", 0, 0, tiled=True)
        routing = jnp.concatenate(
            [own_routes, numer, jnp.zeros((5, tokens), jnp.int32)], axis=0
        )
        routing = lax.all_gather(routing, "seq", axis=1, tiled=True)
        carried = weights
    if halves == 2:
        weights = [[got, swap(again, "dat", 1)] for got, again in zip(weights, carried)]
    else:
        weights = [[got] for got in weights]
    rows = [mine] + [swap(mine, "head", m) for m in range(1, head_count)]
    sums = project(rows, [[own_weights]] + weights, count if split else 1)
    chunk = min(256, expert_gate.shape[2])
    early = max(1, expert_gate.shape[0] * (expert_gate.shape[2] // chunk) * 12 // 16)
    *fetched, mixed = fetch(expert_gate, expert_up, sums[0], chunk, early)
    if split:
        received = swaps(sums, "seq")[1:]
        for part_sum in received:
            mixed = mixed + part_sum.astype(F32)
    else:
        mixed = lax.psum_scatter(mixed, "seq", scatter_dimension=0, tiled=True)

    stream = (residual_in[0].astype(F32) + mixed).astype(BF16)
    own_columns = spread(stream, "seq")
    columns = [own_columns] + [
        [swap(piece, "head", m) for piece in own_columns] for m in range(1, head_count)
    ]
    passes = [[0], list(range(1, head_count))] if head_count > 1 else [[0]]
    fetched_rows = fetch_rows(expert_gate, expert_up, stream, chunk, early, share)
    carried = [routing]
    for i, places in enumerate(passes):
        carried = run_experts(
            [columns[m] for m in places],
            tuple(places),
            gain,
            fetched,
            [] if i else fetched_rows,
            (expert_gate, expert_up),
            tokens,
            count,
            carried,
            i == len(passes) - 1,
        )
    hidden = carried[0]
    return (stream[None], hidden[:, None])


def solution(mesh):
    in_specs = (
        P(("grp", "dat"), "seq", "head"),
        P(("grp", "dat"), "seq", "head"),
        P(("grp", "dat"), "seq", "head"),
        P(("grp", "dat"), "seq", "head"),
        P("head", "seq", None),
        P(),
        P("head", None, "seq"),
        P("head", None, "seq"),
        P(("grp", "dat"), "seq", None),
        P(("grp", "dat"), "seq"),
        P(("grp", "dat")),
    )
    out_specs = (P(("grp", "dat"), "seq", "head"), P("head", ("grp", "dat"), None, "seq"))
    return jax.shard_map(local, mesh=mesh, in_specs=in_specs, out_specs=out_specs, check_vma=False)
```

```python
import functools
import math

import jax
import jax.numpy as jnp
from jax import lax
from jax.experimental import pallas as pl
from jax.experimental.pallas import tpu as pltpu
from jax.sharding import PartitionSpec as P

HEAD_SIZE = 128
QUERY_HEAD_COUNT = 24
KEY_VALUE_HEADS = 4
MOST = 40
EXTRA = 16
ATTENDED_ORDER = (0, 3, 2, 1)
STREAM_ORDER = (0, 3, 1, 2)
EPS = 1e-05
NEG = -1e30
F32 = jnp.float32
BF16 = jnp.bfloat16

VMEM = pl.BlockSpec(memory_space=pltpu.VMEM)
SMEM = pl.BlockSpec(memory_space=pltpu.SMEM)
ANY = pl.BlockSpec(memory_space=pl.ANY)
place = pltpu.with_memory_space_constraint
HBM = pl.BlockSpec(memory_space=pltpu.HBM)


def pairwise(count):
    return count in (1, 2, 4)


def swap(array, axis, step, upward=False):
    count = lax.axis_size(axis)
    pairs = [(i, i ^ step) for i in range(count) if not upward or i < i ^ step]
    return lax.ppermute(array, axis, pairs)


def steps_of(count):
    return [k for k in (2, 3, 1) if k < count]


def shuffled(pieces, order):
    return [pieces[k] for k in order] if len(pieces) == len(order) else list(pieces)


def sorted_back(pieces, order):
    return [pieces[order.index(k)] for k in range(4)] if len(pieces) == len(order) else list(pieces)


def swaps(arrays, axis, upward=False):
    got = {k: swap(arrays[k], axis, k, upward) for k in steps_of(len(arrays))}
    return [arrays[0]] + [got[k] for k in range(1, len(arrays))]


def spread(array, axis, upward=False):
    count = lax.axis_size(axis)
    if pairwise(count):
        return swaps([array] * count, axis, upward)
    return [lax.all_gather(array, axis, axis=0, tiled=True)]


def attention_kernel(shape, lengths, queries, gain_in, routes, numer, *refs):
    tokens, groups, per_group, pieces, split = shape
    kv_refs, refs = refs[:pieces], refs[pieces:]
    gain_out, outs = refs[0], refs[1:]
    rank = lax.axis_index("seq")
    gain_out[...] = gain_in[...]
    flip, valid_len = rank if split else 0, lengths[0]
    width = groups * HEAD_SIZE
    key_parts = [ref[:, :width] for ref in kv_refs]
    value_parts = [ref[:, width:] for ref in kv_refs]
    all_keys = jnp.concatenate(key_parts, axis=0)
    all_values = jnp.concatenate(value_parts, axis=0)
    length = all_keys.shape[0]
    column = lax.broadcasted_iota(jnp.int32, (tokens, length), 1)
    block = lax.div(column, tokens)
    key_pos = lax.bitwise_xor(block, flip) * tokens + (column - block * tokens)
    query_pos = rank * tokens + lax.broadcasted_iota(jnp.int32, (tokens, length), 0)
    allowed = ((key_pos <= query_pos) & (key_pos < valid_len)).astype(F32)
    allowed = jnp.concatenate([allowed] * per_group, axis=0) > 0
    scale = 1.0 / math.sqrt(HEAD_SIZE)
    attended = []
    for g in range(groups):
        heads = [g * per_group + a for a in range(per_group)]
        rows = jnp.concatenate(
            [queries[:, h * HEAD_SIZE : (h + 1) * HEAD_SIZE] for h in heads], axis=0
        )
        lanes = slice(g * HEAD_SIZE, (g + 1) * HEAD_SIZE)
        scores = (
            lax.dot_general(
                rows, all_keys[:, lanes], (((1,), (1,)), ((), ())), preferred_element_type=F32
            )
            * scale
        )
        scores = jnp.where(allowed, scores, NEG)
        top = jnp.max(scores, axis=-1, keepdims=True)
        weights = jnp.where(allowed, jnp.exp(scores - top), 0.0)
        denom = jnp.sum(weights, axis=-1, keepdims=True)
        mixed = jnp.dot(weights.astype(BF16), all_values[:, lanes], preferred_element_type=F32)
        mixed = mixed / denom
        attended += [mixed[a * tokens : (a + 1) * tokens] for a in range(per_group)]
    if not split:
        outs[0][...] = jnp.concatenate(attended, axis=1).astype(BF16)
        return
    count = len(outs)
    part = HEAD_SIZE // count
    shares = [
        jnp.concatenate([o[:, j * part : (j + 1) * part] for o in attended], axis=1).astype(BF16)
        for j in range(count)
    ]
    routing = jnp.concatenate(
        [routes[...], numer[...], jnp.zeros((EXTRA - 3, tokens), jnp.int32)], axis=0
    )
    routing = routing.astype(F32).astype(BF16)
    for k in range(count):
        chosen = shares[k]
        for s in range(1, count):
            chosen = jnp.where(rank == s, shares[s ^ k], chosen)
        outs[k][:tokens, :] = chosen
        outs[k][tokens:, :] = jnp.zeros((EXTRA, chosen.shape[1]), BF16)
        outs[k][tokens:, :tokens] = routing


def attend(lengths, queries, gain, routes, numer, kv_parts, count):
    tokens = queries.shape[0]
    groups = kv_parts[0].shape[1] // (2 * HEAD_SIZE)
    per_group = QUERY_HEAD_COUNT // KEY_VALUE_HEADS
    split = pairwise(count)
    if split:
        out_shape = [
            jax.ShapeDtypeStruct((tokens + EXTRA, queries.shape[1] // count), BF16)
            for _ in range(count)
        ]
    else:
        out_shape = [jax.ShapeDtypeStruct(queries.shape, BF16)]
    length = tokens * count
    limit = min(40 << 20, (4 << 20) + 48 * per_group * tokens * length)
    out_shape = [
        jax.ShapeDtypeStruct(gain.shape, BF16),
    ] + out_shape
    return pl.pallas_call(
        functools.partial(
            attention_kernel, (tokens, groups, per_group, len(kv_parts), split)
        ),
        out_shape=out_shape,
        in_specs=[SMEM] + [VMEM] * (4 + len(kv_parts)),
        out_specs=[VMEM] * len(out_shape),
        compiler_params=pltpu.CompilerParams(vmem_limit_bytes=limit),
        cost_estimate=pl.CostEstimate(
            flops=4 * tokens * length * queries.shape[1],
            bytes_accessed=4 * queries.size + 4 * length * kv_parts[0].shape[1],
            transcendentals=tokens * length * groups * per_group,
        ),
        name="attention",
    )(lengths, queries, gain, routes, numer, *kv_parts)


def prepare_kernel(matrix, queries, keys, values, routes, numer, *refs):
    kv, rows, first_routes, weights = refs[:4]
    columns, sems = refs[4:-1], refs[-1]
    width = keys.shape[1]
    if columns:
        height, share = columns[0].shape
    pairs = [
        (keys, kv.at[:, :width]),
        (values, kv.at[:, width:]),
        (queries, rows),
        (routes, first_routes),
        (numer, weights),
    ]
    head, core = lax.axis_index("head"), lax.axis_index("dat")
    for m, out in enumerate(columns):
        lanes = pl.ds(pl.multiple_of(lax.bitwise_xor(head, m + 1) * share, share), share)
        if out.shape[0] == matrix.shape[0]:
            source = matrix.at[:, lanes]
        else:
            source = matrix.at[pl.ds(pl.multiple_of(core * height, height), height), lanes]
        pairs.insert(2, (source, out))
    copies = [pltpu.make_async_copy(*pair, sems.at[i]) for i, pair in enumerate(pairs)]
    for copy in copies:
        copy.start()
    for copy in copies:
        copy.wait()


def prepare(matrix, queries, keys, values, routes, numer, head_count, halves):
    rows, features = matrix.shape
    tokens = queries.shape[0]
    share = features // head_count
    out_shape = [
        jax.ShapeDtypeStruct((tokens, 2 * keys.shape[1]), BF16),
        jax.ShapeDtypeStruct(queries.shape, BF16),
        jax.ShapeDtypeStruct(routes.shape, jnp.int32),
        jax.ShapeDtypeStruct(numer.shape, jnp.int32),
    ] + [pltpu.VMEM((rows // halves, share), BF16)] * (head_count - 1)
    sources = [matrix, queries, keys, values, routes, numer]
    return pl.pallas_call(
        prepare_kernel,
        out_shape=out_shape,
        in_specs=[HBM] * len(sources),
        out_specs=[VMEM] * len(out_shape),
        scratch_shapes=[pltpu.SemaphoreType.DMA((4 + head_count,))],
        compiler_params=pltpu.CompilerParams(vmem_limit_bytes=8 << 20),
        cost_estimate=pl.CostEstimate(
            flops=0, bytes_accessed=4 * rows * features, transcendentals=0
        ),
        name="prepare",
    )(*[place(source, pltpu.HBM) for source in sources])


def own_columns_kernel(matrix, after, out, sem):
    share = out.shape[1]
    lanes = pl.ds(pl.multiple_of(lax.axis_index("head") * share, share), share)
    copy = pltpu.make_async_copy(matrix.at[:, lanes], out, sem)
    copy.start()
    copy.wait()


def own_columns_of(matrix, share, after):
    rows = matrix.shape[0]
    return pl.pallas_call(
        own_columns_kernel,
        out_shape=jax.ShapeDtypeStruct((rows, share), BF16),
        in_specs=[HBM, ANY],
        out_specs=VMEM,
        scratch_shapes=[pltpu.SemaphoreType.DMA],
        compiler_params=pltpu.CompilerParams(vmem_limit_bytes=4 << 20),
        cost_estimate=pl.CostEstimate(
            flops=0, bytes_accessed=4 * rows * share, transcendentals=0
        ),
        name="own_columns",
    )(place(matrix, pltpu.HBM), after)


def pack_kernel(tokens, pieces, *refs):
    parts, refs = sorted_back(refs[:pieces], ATTENDED_ORDER), refs[pieces:]
    carried = (len(refs) - 3) // 2
    carried_in, packed, route, refs = refs[:carried], refs[carried], refs[carried + 1], refs[carried + 2 :]
    copies = [
        pltpu.make_async_copy(source, out, refs[-1].at[i])
        for i, (source, out) in enumerate(zip(carried_in, refs[:-1]))
    ]
    for copy in copies:
        copy.start()
    for k, ref in enumerate(parts):
        at = slice(k * tokens, (k + 1) * tokens)
        packed[at, :] = ref[:tokens, :]
        route[:, at] = ref[tokens : tokens + 8, :tokens]
    for copy in copies:
        copy.wait()


def pack(parts, tokens, carried):
    width = parts[0].shape[1]
    rows = tokens * len(parts)
    out_shape = [
        jax.ShapeDtypeStruct((rows, width), BF16),
        jax.ShapeDtypeStruct((8, rows), BF16),
        *[jax.ShapeDtypeStruct(array.shape, array.dtype) for array in carried],
    ]
    return pl.pallas_call(
        functools.partial(pack_kernel, tokens, len(parts)),
        out_shape=out_shape,
        in_specs=[VMEM] * len(parts) + [ANY] * len(carried),
        out_specs=[VMEM] * len(out_shape),
        scratch_shapes=[pltpu.SemaphoreType.DMA((max(1, len(carried)),))],
        compiler_params=pltpu.CompilerParams(vmem_limit_bytes=6 << 20),
        name="pack",
    )(*shuffled(parts, ATTENDED_ORDER), *carried)


def project_kernel(parts, halves, *refs):
    rows, refs = refs[:parts], refs[parts:]
    weights = [refs[:1]] + [refs[1 + m * halves : 1 + (m + 1) * halves] for m in range(parts - 1)]
    outs = refs[1 + (parts - 1) * halves :]
    core = lax.axis_index("dat")
    total = None
    for m in range(parts):
        factors = [rows[m][...]]
        if len(weights[m]) > 1:
            half = rows[m].shape[1] // 2
            low, high = factors[0][:, :half], factors[0][:, half:]
            factors = [jnp.where(core == 0, low, high), jnp.where(core == 0, high, low)]
        for factor, weight in zip(factors, weights[m]):
            product = jnp.dot(factor, weight[...], preferred_element_type=F32)
            total = product if total is None else total + product
    at = 0
    for out in outs:
        out[...] = total[at : at + out.shape[0]].astype(out.dtype)
        at += out.shape[0]


def project(rows, weights, pieces):
    parts, (tokens, depth), width = len(rows), rows[0].shape, weights[0][0].shape[1]
    flat_weights = [w for part in weights for w in part]
    return pl.pallas_call(
        functools.partial(project_kernel, parts, len(weights[-1])),
        out_shape=[
            jax.ShapeDtypeStruct((tokens // pieces, width), BF16 if i else F32)
            for i in range(pieces)
        ],
        in_specs=[VMEM] * (parts + len(flat_weights)),
        out_specs=[VMEM] * pieces,
        compiler_params=pltpu.CompilerParams(
            vmem_limit_bytes=min(40 << 20, (4 << 20) + 16 * tokens * width)
        ),
        cost_estimate=pl.CostEstimate(
            flops=2 * tokens * width * parts * depth,
            bytes_accessed=2 * parts * depth * width + 4 * tokens * width,
            transcendentals=0,
        ),
        name="projection",
    )(*rows, *flat_weights)


def fetch_kernel(chunk, gate_hbm, up_hbm, kept, *refs):
    outs, done, sems = refs[:-2], refs[-2], refs[-1]
    per_expert = gate_hbm.shape[2] // chunk
    copies = []
    for step, out in enumerate(outs):
        at = pl.ds((step % per_expert) * chunk, chunk)
        for i, source in enumerate((gate_hbm, up_hbm)):
            copies.append(
                pltpu.make_async_copy(
                    source.at[step // per_expert, :, at], out.at[i], sems.at[step, i]
                )
            )
    for copy in copies:
        copy.start()
    done[...] = kept[...]
    for copy in copies:
        copy.wait()


def fetch(expert_gate, expert_up, kept, chunk, early):
    features = expert_gate.shape[1]
    return pl.pallas_call(
        functools.partial(fetch_kernel, chunk),
        out_shape=[pltpu.VMEM((2, features, chunk), BF16)] * early
        + [
            jax.ShapeDtypeStruct(kept.shape, F32),
        ],
        in_specs=[HBM, HBM, VMEM],
        out_specs=[VMEM] * (early + 1),
        scratch_shapes=[pltpu.SemaphoreType.DMA((early, 2))],
        compiler_params=pltpu.CompilerParams(vmem_limit_bytes=4 << 20 if kept.size < 1 << 20 else 40 << 20),
        cost_estimate=pl.CostEstimate(
            flops=0, bytes_accessed=8 * early * features * chunk, transcendentals=0
        ),
        name="fetch",
    )(place(expert_gate, pltpu.HBM), place(expert_up, pltpu.HBM), kept)


def fetch_rows_kernel(chunk, early, gate_hbm, up_hbm, after, *refs):
    outs, sems = refs[:-1], refs[-1]
    width = outs[0].shape[1]
    per_expert = gate_hbm.shape[2] // chunk
    inner = pl.ds(pl.multiple_of(lax.axis_index("head") * width, width), width)
    copies = []
    for i, out in enumerate(outs):
        step = early + i
        at = pl.ds((step % per_expert) * chunk, chunk)
        for j, source in enumerate((gate_hbm, up_hbm)):
            copies.append(
                pltpu.make_async_copy(
                    source.at[step // per_expert, inner, at], out.at[j], sems.at[i, j]
                )
            )
    for copy in copies:
        copy.start()
    for copy in copies:
        copy.wait()


def fetch_rows(expert_gate, expert_up, after, chunk, early, width):
    experts, _, hidden_units = expert_gate.shape
    late = experts * (hidden_units // chunk) - early
    if not late:
        return []
    return pl.pallas_call(
        functools.partial(fetch_rows_kernel, chunk, early),
        out_shape=[pltpu.VMEM((2, width, chunk), BF16)] * late,
        in_specs=[HBM, HBM, ANY],
        out_specs=[VMEM] * late,
        scratch_shapes=[pltpu.SemaphoreType.DMA((late, 2))],
        compiler_params=pltpu.CompilerParams(vmem_limit_bytes=1 << 20),
        cost_estimate=pl.CostEstimate(
            flops=0, bytes_accessed=8 * late * width * chunk, transcendentals=0
        ),
        name="fetch_rows",
    )(place(expert_gate, pltpu.HBM), place(expert_up, pltpu.HBM), after)


def expert_kernel(shape, *refs):
    tokens, group, places, pieces, experts, slots, chunk, depth, early, ready, flips, first, last = shape
    parts = len(places)
    columns = [
        sorted_back(refs[m * pieces : (m + 1) * pieces], STREAM_ORDER) for m in range(parts)
    ]
    refs = refs[parts * pieces :]
    if first:
        routing, gain, refs = refs[0], refs[1], refs[2:]
    else:
        gain, picks, factors, squares_in, sums_in = refs[:5]
        refs = refs[5:]
    fetched, refs = refs[:early], refs[early:]
    fetched_rows, refs = refs[:ready], refs[ready:]
    gate_hbm, up_hbm, refs = refs[0], refs[1], refs[2:]
    if last:
        hidden, refs = refs[0], refs[1:]
    if first:
        picks, factors, refs = refs[0], refs[1], refs[2:]
    squares, sums, chosen, buffers, sems, out_sems = refs
    flip = lax.axis_index("seq") if flips else 0
    head = lax.axis_index("head")
    width = gain.shape[2]
    features = width * gain.shape[0]
    per_expert = gate_hbm.shape[2] // chunk
    steps = experts * per_expert
    size = group * tokens
    height = group * slots
    at_head = [lax.bitwise_xor(head, m) for m in places]
    inner = [pl.ds(pl.multiple_of(p * width, width), width) for p in at_head]

    def copies(step, slot):
        e, at = step // per_expert, pl.ds((step % per_expert) * chunk, chunk)
        return [
            pltpu.make_async_copy(
                source.at[e, inner[p], at], buffers.at[slot, i, p], sems.at[slot, i, p]
            )
            for p in range(parts)
            for i, source in enumerate((gate_hbm, up_hbm))
        ]

    for slot in range(depth):
        for copy in copies(early + slot, slot):
            copy.start()

    groups = picks.shape[0]
    if first:
        slot_row = lax.broadcasted_iota(jnp.int32, (height, size), 0)
        token_col = lax.broadcasted_iota(jnp.int32, (height, size), 1)
        row_block = lax.div(slot_row, slots)
        row_rank = slot_row - row_block * slots
        col_block = lax.bitwise_xor(lax.div(token_col, tokens), flip)
        same_block = row_block == col_block
        before_row = lax.broadcasted_iota(jnp.int32, (size, size), 0)
        before_col = lax.broadcasted_iota(jnp.int32, (size, size), 1)
        before = (
            (before_row < before_col)
            & (lax.div(before_row, tokens) == lax.div(before_col, tokens))
        ).astype(BF16)
        ranks = lax.broadcasted_iota(jnp.int32, (8, size), 0)
        for g in range(groups):
            route = routing[:, g * size : (g + 1) * size].astype(F32)
            first_route, second_route, weight = route[0:1], route[1:2], route[2:3] / 256.0
            gate_rows = []
            for e in range(experts):
                expert = (head * experts + e).astype(F32)
                gate_rows.append(
                    jnp.where(first_route == expert, weight, 0.0)
                    + jnp.where(second_route == expert, 1.0 - weight, 0.0)
                )
            marked = jnp.zeros((8, size), F32)
            for e in range(experts):
                marked = jnp.where(ranks == e, (gate_rows[e] > 0).astype(F32), marked)
            counted = jnp.dot(marked.astype(BF16), before, preferred_element_type=F32)
            for e in range(experts):
                hit = (
                    same_block
                    & (counted[e : e + 1].astype(jnp.int32) == row_rank)
                    & (gate_rows[e] > 0)
                )
                picks[g, e * height : (e + 1) * height, :] = hit.astype(BF16)
                factors[e, g * height : (g + 1) * height, :] = jnp.sum(
                    jnp.where(hit, gate_rows[e], 0.0), axis=1, keepdims=True
                )
    for g in range(groups):
        total = None
        for p in range(parts):
            if pieces > 1:
                tokens_in = jnp.concatenate([ref[...] for ref in columns[p]], axis=0)
            else:
                tokens_in = columns[p][0][g * size : (g + 1) * size]
            rows = jnp.dot(picks[g], tokens_in, preferred_element_type=F32)
            part = jnp.sum(rows * rows, axis=1, keepdims=True)
            total = part if total is None else total + part
            rows = (rows * gain[at_head[p]].astype(F32)).astype(BF16)
            for e in range(experts):
                chosen[p, e, g * height : (g + 1) * height, :] = rows[
                    e * height : (e + 1) * height
                ]
        for e in range(experts):
            at = slice(g * height, (g + 1) * height)
            here = total[e * height : (e + 1) * height]
            if not first:
                here = here + squares_in[e, at, :]
            squares[e, at, :] = here

    def compute(step, gate_of, up_of):
        e, begin = step // per_expert, (step % per_expert) * chunk
        at = slice(begin, begin + chunk)
        gate_part = up_part = None
        for p in range(parts):
            rows = chosen[p, e]
            a = jnp.dot(rows, gate_of(p), preferred_element_type=F32)
            b = jnp.dot(rows, up_of(p), preferred_element_type=F32)
            gate_part = a if gate_part is None else gate_part + a
            up_part = b if up_part is None else up_part + b
        if not first:
            gate_part = gate_part + sums_in[0, e, :, at].astype(F32)
            up_part = up_part + sums_in[1, e, :, at].astype(F32)
        if not last:
            sums[0, e, :, at] = gate_part.astype(BF16)
            sums[1, e, :, at] = up_part.astype(BF16)
            return
        scale = lax.rsqrt(squares[e] / features + EPS)
        gate_part, up_part = gate_part * scale, up_part * scale
        result = factors[e] * (gate_part / (1.0 + jnp.exp(-gate_part)) * up_part)
        sums[e, :, at] = result.astype(BF16)
        store(step).start()

    def store(step):
        e, at = step // per_expert, pl.ds((step % per_expert) * chunk, chunk)
        return pltpu.make_async_copy(sums.at[e, :, at], hidden.at[e, :, at], out_sems.at[step])

    late = list(range(early + ready, steps))
    soon = len(late) - depth if late else 0
    order = [*range(early // 2), *late[:soon], *range(early // 2, early + ready), *late[soon:]]
    for step in order:
        if step < early:
            ref = fetched[step]
            compute(step, lambda p: ref[0, inner[p], :], lambda p: ref[1, inner[p], :])
            continue
        if step < early + ready:
            ref = fetched_rows[step - early]
            compute(step, lambda p: ref[0], lambda p: ref[1])
            continue
        slot = (step - early) % depth
        for copy in copies(step, slot):
            copy.wait()
        compute(
            step, lambda p: buffers[slot, 0, p], lambda p: buffers[slot, 1, p]
        )
        if step + depth < steps:
            for copy in copies(step + depth, slot):
                copy.start()
    if last:
        for step in range(steps):
            store(step).wait()


def run_experts(
    columns, places, gain, fetched, fetched_rows, matrices, tokens, count, carried, last
):
    first = len(carried) == 1
    parts, pieces = len(columns), len(columns[0])
    experts, features, hidden_units = matrices[0].shape
    width = gain.shape[2]
    early, chunk = len(fetched), fetched[0].shape[2]
    ready = len(fetched_rows)
    steps = experts * (hidden_units // chunk)
    depth = min(3, steps - early - ready)
    group = min(4, count)
    slots = MOST * count
    shape = (tokens, group, places, pieces, experts, MOST, chunk, depth, early, ready, pairwise(count), first, last)
    flat = [p for part in columns for p in shuffled(part, STREAM_ORDER)]
    routing, carried = (carried, []) if first else ([], carried)
    kept = [
        jax.ShapeDtypeStruct((count // group, experts * group * MOST, group * tokens), BF16),
        jax.ShapeDtypeStruct((experts, slots, 1), F32),
    ]
    passed = [
        jax.ShapeDtypeStruct((experts, slots, 1), F32),
        jax.ShapeDtypeStruct((2, experts, slots, hidden_units), BF16),
    ]
    out_shape = [jax.ShapeDtypeStruct((experts, slots, hidden_units), BF16)] if last else []
    scratch = []
    for wanted, shapes in ((first, kept), (True, passed)):
        if wanted and last:
            scratch += [pltpu.VMEM(a.shape, a.dtype) for a in shapes]
        elif wanted:
            out_shape += shapes
    if last:
        scratch[-1] = pltpu.VMEM((experts, slots, hidden_units), BF16)
    small = count <= 4
    limit = (6 << 20) if small and not last else (9 << 20) if small else 44 << 20
    return pl.pallas_call(
        functools.partial(expert_kernel, shape),
        out_shape=out_shape,
        in_specs=[VMEM] * (len(flat) + len(routing) + 1 + len(carried) + early + ready)
        + [HBM, HBM],
        out_specs=[ANY] * last + [VMEM] * (len(out_shape) - last),
        scratch_shapes=scratch
        + [
            pltpu.VMEM((parts, experts, slots, width), BF16),
            pltpu.VMEM((max(depth, 1), 2, parts, width if depth else 16, chunk), BF16),
            pltpu.SemaphoreType.DMA((max(depth, 1), 2, parts)),
            pltpu.SemaphoreType.DMA((steps,)),
        ],
        compiler_params=pltpu.CompilerParams(vmem_limit_bytes=limit),
        cost_estimate=pl.CostEstimate(
            flops=4 * experts * slots * width * parts * hidden_units,
            bytes_accessed=2 * matrices[0].size,
            transcendentals=experts * slots * hidden_units,
        ),
        name="experts",
    )(
        *flat,
        *routing,
        gain,
        *carried,
        *[place(part, pltpu.VMEM) for part in (*fetched, *fetched_rows)],
        *[place(matrix, pltpu.HBM) for matrix in matrices],
    )


def local(
    queries,
    keys,
    values,
    residual_in,
    out_proj,
    norm_gain,
    expert_gate,
    expert_up,
    routes,
    gate_numer,
    sequence_lengths,
):
    tokens = queries.shape[1]
    count = lax.axis_size("seq")
    head_count = lax.axis_size("head")
    split = pairwise(count)
    share = residual_in.shape[2]
    features = out_proj.shape[2]
    heads, part, _ = out_proj.shape

    matrix = out_proj.reshape(heads * part, features)
    halves = 2 if lax.axis_size("dat") == 2 and matrix.shape[0] % 32 == 0 else 1
    own_kv, rows, own_routes, numer, *weights = prepare(
        matrix, queries[0], keys[0], values[0], routes[0].T, gate_numer, head_count, halves
    )

    weights = [swap(weights[m - 1], "head", m) for m in range(1, head_count)]

    kv_parts = spread(own_kv, "seq")
    gain = norm_gain.reshape(head_count, 1, share)

    gain, *attended = attend(
        sequence_lengths, rows, gain, own_routes, numer, kv_parts, count
    )
    if split:
        attended = swaps(attended, "seq")
        mine, routing, *carried = pack(attended, tokens, weights if halves == 2 else [])
    else:
        shares = attended[0].reshape(tokens, heads, count, part).transpose(2, 0, 1, 3)
        shares = shares.reshape(count * tokens, heads * part)
        mine = lax.all_to_all(shares, "seq", 0, 0, tiled=True)
        routing = jnp.concatenate(
            [own_routes, numer, jnp.zeros((5, tokens), jnp.int32)], axis=0
        )
        routing = lax.all_gather(routing, "seq", axis=1, tiled=True)
        carried = weights
    if halves == 2:
        weights = [[got, swap(again, "dat", 1)] for got, again in zip(weights, carried)]
    else:
        weights = [[got] for got in weights]
    own_weights = own_columns_of(matrix, share, mine)
    rows = [mine] + [swap(mine, "head", m) for m in range(1, head_count)]
    sums = project(rows, [[own_weights]] + weights, count if split else 1)
    chunk = min(256, expert_gate.shape[2])
    early = max(1, expert_gate.shape[0] * (expert_gate.shape[2] // chunk) * 12 // 16)
    *fetched, mixed = fetch(expert_gate, expert_up, sums[0], chunk, early)
    if split:
        received = swaps(sums, "seq")[1:]
        for part_sum in received:
            mixed = mixed + part_sum.astype(F32)
    else:
        mixed = lax.psum_scatter(mixed, "seq", scatter_dimension=0, tiled=True)

    stream = (residual_in[0].astype(F32) + mixed).astype(BF16)
    own_columns = spread(stream, "seq")
    columns = [own_columns] + [
        [swap(piece, "head", m) for piece in own_columns] for m in range(1, head_count)
    ]
    passes = [[0], list(range(1, head_count))] if head_count > 1 else [[0]]
    fetched_rows = fetch_rows(expert_gate, expert_up, stream, chunk, early, share)
    carried = [routing]
    for i, places in enumerate(passes):
        carried = run_experts(
            [columns[m] for m in places],
            tuple(places),
            gain,
            fetched,
            [] if i else fetched_rows,
            (expert_gate, expert_up),
            tokens,
            count,
            carried,
            i == len(passes) - 1,
        )
    hidden = carried[0]
    return (stream[None], hidden[:, None])


def solution(mesh):
    in_specs = (
        P(("grp", "dat"), "seq", "head"),
        P(("grp", "dat"), "seq", "head"),
        P(("grp", "dat"), "seq", "head"),
        P(("grp", "dat"), "seq", "head"),
        P("head", "seq", None),
        P(),
        P("head", None, "seq"),
        P("head", None, "seq"),
        P(("grp", "dat"), "seq", None),
        P(("grp", "dat"), "seq"),
        P(("grp", "dat")),
    )
    out_specs = (P(("grp", "dat"), "seq", "head"), P("head", ("grp", "dat"), None, "seq"))
    return jax.shard_map(local, mesh=mesh, in_specs=in_specs, out_specs=out_specs, check_vma=False)
```

```python
import functools
import math

import jax
import jax.numpy as jnp
from jax import lax
from jax.experimental import pallas as pl
from jax.experimental.pallas import tpu as pltpu
from jax.sharding import PartitionSpec as P

HEAD_SIZE = 128
QUERY_HEAD_COUNT = 24
KEY_VALUE_HEADS = 4
MOST = 40
EXTRA = 16
ATTENDED_ORDER = (0, 3, 2, 1)
STREAM_ORDER = (0, 3, 1, 2)
EPS = 1e-05
NEG = -1e30
F32 = jnp.float32
BF16 = jnp.bfloat16

VMEM = pl.BlockSpec(memory_space=pltpu.VMEM)
SMEM = pl.BlockSpec(memory_space=pltpu.SMEM)
ANY = pl.BlockSpec(memory_space=pl.ANY)
place = pltpu.with_memory_space_constraint
HBM = pl.BlockSpec(memory_space=pltpu.HBM)


def pairwise(count):
    return count in (1, 2, 4)


def swap(array, axis, step, upward=False):
    count = lax.axis_size(axis)
    pairs = [(i, i ^ step) for i in range(count) if not upward or i < i ^ step]
    return lax.ppermute(array, axis, pairs)


def steps_of(count):
    return [k for k in (2, 3, 1) if k < count]


def shuffled(pieces, order):
    return [pieces[k] for k in order] if len(pieces) == len(order) else list(pieces)


def sorted_back(pieces, order):
    return [pieces[order.index(k)] for k in range(4)] if len(pieces) == len(order) else list(pieces)


def swaps(arrays, axis, upward=False):
    got = {k: swap(arrays[k], axis, k, upward) for k in steps_of(len(arrays))}
    return [arrays[0]] + [got[k] for k in range(1, len(arrays))]


def spread(array, axis, upward=False):
    count = lax.axis_size(axis)
    if pairwise(count):
        return swaps([array] * count, axis, upward)
    return [lax.all_gather(array, axis, axis=0, tiled=True)]


def attention_kernel(shape, lengths, queries, gain_in, routes, numer, *refs):
    tokens, groups, per_group, pieces, split = shape
    kv_refs, refs = refs[:pieces], refs[pieces:]
    gain_out, outs = refs[0], refs[1:]
    rank = lax.axis_index("seq")
    gain_out[...] = gain_in[...]
    flip, valid_len = rank if split else 0, lengths[0]
    width = groups * HEAD_SIZE
    key_parts = [ref[:, :width] for ref in kv_refs]
    value_parts = [ref[:, width:] for ref in kv_refs]
    all_keys = jnp.concatenate(key_parts, axis=0)
    all_values = jnp.concatenate(value_parts, axis=0)
    length = all_keys.shape[0]
    column = lax.broadcasted_iota(jnp.int32, (tokens, length), 1)
    block = lax.div(column, tokens)
    key_pos = lax.bitwise_xor(block, flip) * tokens + (column - block * tokens)
    query_pos = rank * tokens + lax.broadcasted_iota(jnp.int32, (tokens, length), 0)
    allowed = ((key_pos <= query_pos) & (key_pos < valid_len)).astype(F32)
    allowed = jnp.concatenate([allowed] * per_group, axis=0) > 0
    scale = 1.0 / math.sqrt(HEAD_SIZE)
    attended = []
    for g in range(groups):
        heads = [g * per_group + a for a in range(per_group)]
        rows = jnp.concatenate(
            [queries[:, h * HEAD_SIZE : (h + 1) * HEAD_SIZE] for h in heads], axis=0
        )
        lanes = slice(g * HEAD_SIZE, (g + 1) * HEAD_SIZE)
        scores = (
            lax.dot_general(
                rows, all_keys[:, lanes], (((1,), (1,)), ((), ())), preferred_element_type=F32
            )
            * scale
        )
        scores = jnp.where(allowed, scores, NEG)
        top = jnp.max(scores, axis=-1, keepdims=True)
        weights = jnp.where(allowed, jnp.exp(scores - top), 0.0)
        denom = jnp.sum(weights, axis=-1, keepdims=True)
        mixed = jnp.dot(weights.astype(BF16), all_values[:, lanes], preferred_element_type=F32)
        mixed = mixed / denom
        attended += [mixed[a * tokens : (a + 1) * tokens] for a in range(per_group)]
    if not split:
        outs[0][...] = jnp.concatenate(attended, axis=1).astype(BF16)
        return
    count = len(outs)
    part = HEAD_SIZE // count
    shares = [
        jnp.concatenate([o[:, j * part : (j + 1) * part] for o in attended], axis=1).astype(BF16)
        for j in range(count)
    ]
    routing = jnp.concatenate(
        [routes[...], numer[...], jnp.zeros((EXTRA - 3, tokens), jnp.int32)], axis=0
    )
    routing = routing.astype(F32).astype(BF16)
    for k in range(count):
        chosen = shares[k]
        for s in range(1, count):
            chosen = jnp.where(rank == s, shares[s ^ k], chosen)
        outs[k][:tokens, :] = chosen
        outs[k][tokens:, :] = jnp.zeros((EXTRA, chosen.shape[1]), BF16)
        outs[k][tokens:, :tokens] = routing


def attend(lengths, queries, gain, routes, numer, kv_parts, count):
    tokens = queries.shape[0]
    groups = kv_parts[0].shape[1] // (2 * HEAD_SIZE)
    per_group = QUERY_HEAD_COUNT // KEY_VALUE_HEADS
    split = pairwise(count)
    if split:
        out_shape = [
            jax.ShapeDtypeStruct((tokens + EXTRA, queries.shape[1] // count), BF16)
            for _ in range(count)
        ]
    else:
        out_shape = [jax.ShapeDtypeStruct(queries.shape, BF16)]
    length = tokens * count
    limit = min(40 << 20, (4 << 20) + 48 * per_group * tokens * length)
    out_shape = [
        jax.ShapeDtypeStruct(gain.shape, BF16),
    ] + out_shape
    return pl.pallas_call(
        functools.partial(
            attention_kernel, (tokens, groups, per_group, len(kv_parts), split)
        ),
        out_shape=out_shape,
        in_specs=[SMEM] + [VMEM] * (4 + len(kv_parts)),
        out_specs=[VMEM] * len(out_shape),
        compiler_params=pltpu.CompilerParams(vmem_limit_bytes=limit),
        cost_estimate=pl.CostEstimate(
            flops=4 * tokens * length * queries.shape[1],
            bytes_accessed=4 * queries.size + 4 * length * kv_parts[0].shape[1],
            transcendentals=tokens * length * groups * per_group,
        ),
        name="attention",
    )(lengths, queries, gain, routes, numer, *kv_parts)


def prepare_kernel(matrix, queries, keys, values, routes, numer, *refs):
    kv, rows, first_routes, weights = refs[:4]
    columns, sems = refs[4:-1], refs[-1]
    width = keys.shape[1]
    if columns:
        height, share = columns[0].shape
    pairs = [
        (keys, kv.at[:, :width]),
        (values, kv.at[:, width:]),
        (queries, rows),
        (routes, first_routes),
        (numer, weights),
    ]
    head, core = lax.axis_index("head"), lax.axis_index("dat")
    for m, out in enumerate(columns):
        lanes = pl.ds(pl.multiple_of(lax.bitwise_xor(head, m + 1) * share, share), share)
        if out.shape[0] == matrix.shape[0]:
            source = matrix.at[:, lanes]
        else:
            source = matrix.at[pl.ds(pl.multiple_of(core * height, height), height), lanes]
        pairs.insert(2, (source, out))
    copies = [pltpu.make_async_copy(*pair, sems.at[i]) for i, pair in enumerate(pairs)]
    for copy in copies:
        copy.start()
    for copy in copies:
        copy.wait()


def prepare(matrix, queries, keys, values, routes, numer, head_count, halves):
    rows, features = matrix.shape
    tokens = queries.shape[0]
    share = features // head_count
    out_shape = [
        jax.ShapeDtypeStruct((tokens, 2 * keys.shape[1]), BF16),
        jax.ShapeDtypeStruct(queries.shape, BF16),
        jax.ShapeDtypeStruct(routes.shape, jnp.int32),
        jax.ShapeDtypeStruct(numer.shape, jnp.int32),
    ] + [pltpu.VMEM((rows // halves, share), BF16)] * (head_count - 1)
    sources = [matrix, queries, keys, values, routes, numer]
    return pl.pallas_call(
        prepare_kernel,
        out_shape=out_shape,
        in_specs=[HBM] * len(sources),
        out_specs=[VMEM] * len(out_shape),
        scratch_shapes=[pltpu.SemaphoreType.DMA((4 + head_count,))],
        compiler_params=pltpu.CompilerParams(vmem_limit_bytes=8 << 20),
        cost_estimate=pl.CostEstimate(
            flops=0, bytes_accessed=4 * rows * features, transcendentals=0
        ),
        name="prepare",
    )(*[place(source, pltpu.HBM) for source in sources])


def own_columns_kernel(matrix, after, out, sem):
    share = out.shape[1]
    lanes = pl.ds(pl.multiple_of(lax.axis_index("head") * share, share), share)
    copy = pltpu.make_async_copy(matrix.at[:, lanes], out, sem)
    copy.start()
    copy.wait()


def own_columns_of(matrix, share, after):
    rows = matrix.shape[0]
    return pl.pallas_call(
        own_columns_kernel,
        out_shape=jax.ShapeDtypeStruct((rows, share), BF16),
        in_specs=[HBM, ANY],
        out_specs=VMEM,
        scratch_shapes=[pltpu.SemaphoreType.DMA],
        compiler_params=pltpu.CompilerParams(vmem_limit_bytes=4 << 20),
        cost_estimate=pl.CostEstimate(
            flops=0, bytes_accessed=4 * rows * share, transcendentals=0
        ),
        name="own_columns",
    )(place(matrix, pltpu.HBM), after)


def pack_kernel(tokens, pieces, *refs):
    parts, refs = sorted_back(refs[:pieces], ATTENDED_ORDER), refs[pieces:]
    carried = (len(refs) - 4) // 2
    carried_in, refs = refs[:carried], refs[carried:]
    packed, others, route, refs = refs[0], refs[1], refs[2], refs[3:]
    copies = [
        pltpu.make_async_copy(source, out, refs[-1].at[i])
        for i, (source, out) in enumerate(zip(carried_in, refs[:-1]))
    ]
    for copy in copies:
        copy.start()
    for k, ref in enumerate(parts):
        at = slice(k * tokens, (k + 1) * tokens)
        packed[at, :] = ref[:tokens, :]
        if k:
            others[(k - 1) * tokens : k * tokens, :] = ref[:tokens, :]
        route[:, at] = ref[tokens : tokens + 8, :tokens]
    for copy in copies:
        copy.wait()


def pack(parts, tokens, carried):
    width = parts[0].shape[1]
    rows = tokens * len(parts)
    out_shape = [
        jax.ShapeDtypeStruct((rows, width), BF16),
        jax.ShapeDtypeStruct((max(rows - tokens, tokens), width), BF16),
        jax.ShapeDtypeStruct((8, rows), BF16),
        *[jax.ShapeDtypeStruct(array.shape, array.dtype) for array in carried],
    ]
    return pl.pallas_call(
        functools.partial(pack_kernel, tokens, len(parts)),
        out_shape=out_shape,
        in_specs=[VMEM] * len(parts) + [ANY] * len(carried),
        out_specs=[VMEM] * len(out_shape),
        scratch_shapes=[pltpu.SemaphoreType.DMA((max(1, len(carried)),))],
        compiler_params=pltpu.CompilerParams(vmem_limit_bytes=6 << 20),
        name="pack",
    )(*shuffled(parts, ATTENDED_ORDER), *carried)


def project_kernel(parts, halves, sent, tokens, *refs):
    rows, refs = [refs[:1]], refs[1:]
    for _ in range(1, parts):
        rows.append(refs[:sent])
        refs = refs[sent:]
    weights = [refs[:1]] + [refs[1 + m * halves : 1 + (m + 1) * halves] for m in range(parts - 1)]
    outs = refs[1 + (parts - 1) * halves :]
    core = lax.axis_index("dat")
    total = None
    for m in range(parts):
        pieces = [ref[...] for ref in rows[m]]
        if len(pieces) > 1:
            pieces[0] = pieces[0][:tokens]
        factors = [jnp.concatenate(pieces, axis=0)]
        if len(weights[m]) > 1:
            half = factors[0].shape[1] // 2
            low, high = factors[0][:, :half], factors[0][:, half:]
            factors = [jnp.where(core == 0, low, high), jnp.where(core == 0, high, low)]
        for factor, weight in zip(factors, weights[m]):
            product = jnp.dot(factor, weight[...], preferred_element_type=F32)
            total = product if total is None else total + product
    at = 0
    for out in outs:
        out[...] = total[at : at + out.shape[0]].astype(out.dtype)
        at += out.shape[0]


def project(rows, weights, pieces):
    parts, (tokens, depth), width = len(rows), rows[0][0].shape, weights[0][0].shape[1]
    flat = [piece for part in rows for piece in part]
    flat_weights = [w for part in weights for w in part]
    return pl.pallas_call(
        functools.partial(
            project_kernel, parts, len(weights[-1]), len(rows[-1]), tokens // pieces
        ),
        out_shape=[
            jax.ShapeDtypeStruct((tokens // pieces, width), BF16 if i else F32)
            for i in range(pieces)
        ],
        in_specs=[VMEM] * (len(flat) + len(flat_weights)),
        out_specs=[VMEM] * pieces,
        compiler_params=pltpu.CompilerParams(
            vmem_limit_bytes=min(40 << 20, (4 << 20) + 16 * tokens * width)
        ),
        cost_estimate=pl.CostEstimate(
            flops=2 * tokens * width * parts * depth,
            bytes_accessed=2 * parts * depth * width + 4 * tokens * width,
            transcendentals=0,
        ),
        name="projection",
    )(*flat, *flat_weights)


def fetch_kernel(chunk, gate_hbm, up_hbm, kept, *refs):
    outs, done, sems = refs[:-2], refs[-2], refs[-1]
    per_expert = gate_hbm.shape[2] // chunk
    copies = []
    for step, out in enumerate(outs):
        at = pl.ds((step % per_expert) * chunk, chunk)
        for i, source in enumerate((gate_hbm, up_hbm)):
            copies.append(
                pltpu.make_async_copy(
                    source.at[step // per_expert, :, at], out.at[i], sems.at[step, i]
                )
            )
    for copy in copies:
        copy.start()
    done[...] = kept[...]
    for copy in copies:
        copy.wait()


def fetch(expert_gate, expert_up, kept, chunk, early):
    features = expert_gate.shape[1]
    return pl.pallas_call(
        functools.partial(fetch_kernel, chunk),
        out_shape=[pltpu.VMEM((2, features, chunk), BF16)] * early
        + [
            jax.ShapeDtypeStruct(kept.shape, F32),
        ],
        in_specs=[HBM, HBM, VMEM],
        out_specs=[VMEM] * (early + 1),
        scratch_shapes=[pltpu.SemaphoreType.DMA((early, 2))],
        compiler_params=pltpu.CompilerParams(vmem_limit_bytes=4 << 20 if kept.size < 1 << 20 else 40 << 20),
        cost_estimate=pl.CostEstimate(
            flops=0, bytes_accessed=8 * early * features * chunk, transcendentals=0
        ),
        name="fetch",
    )(place(expert_gate, pltpu.HBM), place(expert_up, pltpu.HBM), kept)


def fetch_rows_kernel(chunk, early, gate_hbm, up_hbm, after, *refs):
    outs, sems = refs[:-1], refs[-1]
    width = outs[0].shape[1]
    per_expert = gate_hbm.shape[2] // chunk
    inner = pl.ds(pl.multiple_of(lax.axis_index("head") * width, width), width)
    copies = []
    for i, out in enumerate(outs):
        step = early + i
        at = pl.ds((step % per_expert) * chunk, chunk)
        for j, source in enumerate((gate_hbm, up_hbm)):
            copies.append(
                pltpu.make_async_copy(
                    source.at[step // per_expert, inner, at], out.at[j], sems.at[i, j]
                )
            )
    for copy in copies:
        copy.start()
    for copy in copies:
        copy.wait()


def fetch_rows(expert_gate, expert_up, after, chunk, early, width):
    experts, _, hidden_units = expert_gate.shape
    late = experts * (hidden_units // chunk) - early
    if not late:
        return []
    return pl.pallas_call(
        functools.partial(fetch_rows_kernel, chunk, early),
        out_shape=[pltpu.VMEM((2, width, chunk), BF16)] * late,
        in_specs=[HBM, HBM, ANY],
        out_specs=[VMEM] * late,
        scratch_shapes=[pltpu.SemaphoreType.DMA((late, 2))],
        compiler_params=pltpu.CompilerParams(vmem_limit_bytes=1 << 20),
        cost_estimate=pl.CostEstimate(
            flops=0, bytes_accessed=8 * late * width * chunk, transcendentals=0
        ),
        name="fetch_rows",
    )(place(expert_gate, pltpu.HBM), place(expert_up, pltpu.HBM), after)


def expert_kernel(shape, *refs):
    tokens, group, places, pieces, experts, slots, chunk, depth, early, ready, flips, first, last = shape
    parts = len(places)
    columns = [
        sorted_back(refs[m * pieces : (m + 1) * pieces], STREAM_ORDER) for m in range(parts)
    ]
    refs = refs[parts * pieces :]
    if first:
        routing, gain, refs = refs[0], refs[1], refs[2:]
    else:
        gain, picks, factors, squares_in, sums_in = refs[:5]
        refs = refs[5:]
    fetched, refs = refs[:early], refs[early:]
    fetched_rows, refs = refs[:ready], refs[ready:]
    gate_hbm, up_hbm, refs = refs[0], refs[1], refs[2:]
    if last:
        hidden, refs = refs[0], refs[1:]
    if first:
        picks, factors, refs = refs[0], refs[1], refs[2:]
    squares, sums, chosen, buffers, sems, out_sems = refs
    flip = lax.axis_index("seq") if flips else 0
    head = lax.axis_index("head")
    width = gain.shape[2]
    features = width * gain.shape[0]
    per_expert = gate_hbm.shape[2] // chunk
    steps = experts * per_expert
    size = group * tokens
    height = group * slots
    at_head = [lax.bitwise_xor(head, m) for m in places]
    inner = [pl.ds(pl.multiple_of(p * width, width), width) for p in at_head]

    def copies(step, slot):
        e, at = step // per_expert, pl.ds((step % per_expert) * chunk, chunk)
        return [
            pltpu.make_async_copy(
                source.at[e, inner[p], at], buffers.at[slot, i, p], sems.at[slot, i, p]
            )
            for p in range(parts)
            for i, source in enumerate((gate_hbm, up_hbm))
        ]

    for slot in range(depth):
        for copy in copies(early + slot, slot):
            copy.start()

    groups = picks.shape[0]
    if first:
        slot_row = lax.broadcasted_iota(jnp.int32, (height, size), 0)
        token_col = lax.broadcasted_iota(jnp.int32, (height, size), 1)
        row_block = lax.div(slot_row, slots)
        row_rank = slot_row - row_block * slots
        col_block = lax.bitwise_xor(lax.div(token_col, tokens), flip)
        same_block = row_block == col_block
        before_row = lax.broadcasted_iota(jnp.int32, (size, size), 0)
        before_col = lax.broadcasted_iota(jnp.int32, (size, size), 1)
        before = (
            (before_row < before_col)
            & (lax.div(before_row, tokens) == lax.div(before_col, tokens))
        ).astype(BF16)
        ranks = lax.broadcasted_iota(jnp.int32, (8, size), 0)
        for g in range(groups):
            route = routing[:, g * size : (g + 1) * size].astype(F32)
            first_route, second_route, weight = route[0:1], route[1:2], route[2:3] / 256.0
            gate_rows = []
            for e in range(experts):
                expert = (head * experts + e).astype(F32)
                gate_rows.append(
                    jnp.where(first_route == expert, weight, 0.0)
                    + jnp.where(second_route == expert, 1.0 - weight, 0.0)
                )
            marked = jnp.zeros((8, size), F32)
            for e in range(experts):
                marked = jnp.where(ranks == e, (gate_rows[e] > 0).astype(F32), marked)
            counted = jnp.dot(marked.astype(BF16), before, preferred_element_type=F32)
            for e in range(experts):
                hit = (
                    same_block
                    & (counted[e : e + 1].astype(jnp.int32) == row_rank)
                    & (gate_rows[e] > 0)
                )
                picks[g, e * height : (e + 1) * height, :] = hit.astype(BF16)
                factors[e, g * height : (g + 1) * height, :] = jnp.sum(
                    jnp.where(hit, gate_rows[e], 0.0), axis=1, keepdims=True
                )
    for g in range(groups):
        total = None
        for p in range(parts):
            if pieces > 1:
                tokens_in = jnp.concatenate([ref[...] for ref in columns[p]], axis=0)
            else:
                tokens_in = columns[p][0][g * size : (g + 1) * size]
            rows = jnp.dot(picks[g], tokens_in, preferred_element_type=F32)
            part = jnp.sum(rows * rows, axis=1, keepdims=True)
            total = part if total is None else total + part
            rows = (rows * gain[at_head[p]].astype(F32)).astype(BF16)
            for e in range(experts):
                chosen[p, e, g * height : (g + 1) * height, :] = rows[
                    e * height : (e + 1) * height
                ]
        for e in range(experts):
            at = slice(g * height, (g + 1) * height)
            here = total[e * height : (e + 1) * height]
            if not first:
                here = here + squares_in[e, at, :]
            squares[e, at, :] = here

    def compute(step, gate_of, up_of):
        e, begin = step // per_expert, (step % per_expert) * chunk
        at = slice(begin, begin + chunk)
        gate_part = up_part = None
        for p in range(parts):
            rows = chosen[p, e]
            a = jnp.dot(rows, gate_of(p), preferred_element_type=F32)
            b = jnp.dot(rows, up_of(p), preferred_element_type=F32)
            gate_part = a if gate_part is None else gate_part + a
            up_part = b if up_part is None else up_part + b
        if not first:
            gate_part = gate_part + sums_in[0, e, :, at].astype(F32)
            up_part = up_part + sums_in[1, e, :, at].astype(F32)
        if not last:
            sums[0, e, :, at] = gate_part.astype(BF16)
            sums[1, e, :, at] = up_part.astype(BF16)
            return
        scale = lax.rsqrt(squares[e] / features + EPS)
        gate_part, up_part = gate_part * scale, up_part * scale
        result = factors[e] * (gate_part / (1.0 + jnp.exp(-gate_part)) * up_part)
        sums[e, :, at] = result.astype(BF16)
        store(step).start()

    def store(step):
        e, at = step // per_expert, pl.ds((step % per_expert) * chunk, chunk)
        return pltpu.make_async_copy(sums.at[e, :, at], hidden.at[e, :, at], out_sems.at[step])

    late = list(range(early + ready, steps))
    soon = len(late) - depth if late else 0
    order = [*range(early // 2), *late[:soon], *range(early // 2, early + ready), *late[soon:]]
    for step in order:
        if step < early:
            ref = fetched[step]
            compute(step, lambda p: ref[0, inner[p], :], lambda p: ref[1, inner[p], :])
            continue
        if step < early + ready:
            ref = fetched_rows[step - early]
            compute(step, lambda p: ref[0], lambda p: ref[1])
            continue
        slot = (step - early) % depth
        for copy in copies(step, slot):
            copy.wait()
        compute(
            step, lambda p: buffers[slot, 0, p], lambda p: buffers[slot, 1, p]
        )
        if step + depth < steps:
            for copy in copies(step + depth, slot):
                copy.start()
    if last:
        for step in range(steps):
            store(step).wait()


def run_experts(
    columns, places, gain, fetched, fetched_rows, matrices, tokens, count, carried, last
):
    first = len(carried) == 1
    parts, pieces = len(columns), len(columns[0])
    experts, features, hidden_units = matrices[0].shape
    width = gain.shape[2]
    early, chunk = len(fetched), fetched[0].shape[2]
    ready = len(fetched_rows)
    steps = experts * (hidden_units // chunk)
    depth = min(3, steps - early - ready)
    group = min(4, count)
    slots = MOST * count
    shape = (tokens, group, places, pieces, experts, MOST, chunk, depth, early, ready, pairwise(count), first, last)
    flat = [p for part in columns for p in shuffled(part, STREAM_ORDER)]
    routing, carried = (carried, []) if first else ([], carried)
    kept = [
        jax.ShapeDtypeStruct((count // group, experts * group * MOST, group * tokens), BF16),
        jax.ShapeDtypeStruct((experts, slots, 1), F32),
    ]
    passed = [
        jax.ShapeDtypeStruct((experts, slots, 1), F32),
        jax.ShapeDtypeStruct((2, experts, slots, hidden_units), BF16),
    ]
    out_shape = [jax.ShapeDtypeStruct((experts, slots, hidden_units), BF16)] if last else []
    scratch = []
    for wanted, shapes in ((first, kept), (True, passed)):
        if wanted and last:
            scratch += [pltpu.VMEM(a.shape, a.dtype) for a in shapes]
        elif wanted:
            out_shape += shapes
    if last:
        scratch[-1] = pltpu.VMEM((experts, slots, hidden_units), BF16)
    small = count <= 4
    limit = (6 << 20) if small and not last else (9 << 20) if small else 44 << 20
    return pl.pallas_call(
        functools.partial(expert_kernel, shape),
        out_shape=out_shape,
        in_specs=[VMEM] * (len(flat) + len(routing) + 1 + len(carried) + early + ready)
        + [HBM, HBM],
        out_specs=[ANY] * last + [VMEM] * (len(out_shape) - last),
        scratch_shapes=scratch
        + [
            pltpu.VMEM((parts, experts, slots, width), BF16),
            pltpu.VMEM((max(depth, 1), 2, parts, width if depth else 16, chunk), BF16),
            pltpu.SemaphoreType.DMA((max(depth, 1), 2, parts)),
            pltpu.SemaphoreType.DMA((steps,)),
        ],
        compiler_params=pltpu.CompilerParams(vmem_limit_bytes=limit),
        cost_estimate=pl.CostEstimate(
            flops=4 * experts * slots * width * parts * hidden_units,
            bytes_accessed=2 * matrices[0].size,
            transcendentals=experts * slots * hidden_units,
        ),
        name="experts",
    )(
        *flat,
        *routing,
        gain,
        *carried,
        *[place(part, pltpu.VMEM) for part in (*fetched, *fetched_rows)],
        *[place(matrix, pltpu.HBM) for matrix in matrices],
    )


def local(
    queries,
    keys,
    values,
    residual_in,
    out_proj,
    norm_gain,
    expert_gate,
    expert_up,
    routes,
    gate_numer,
    sequence_lengths,
):
    tokens = queries.shape[1]
    count = lax.axis_size("seq")
    head_count = lax.axis_size("head")
    split = pairwise(count)
    share = residual_in.shape[2]
    features = out_proj.shape[2]
    heads, part, _ = out_proj.shape

    matrix = out_proj.reshape(heads * part, features)
    halves = 2 if lax.axis_size("dat") == 2 and matrix.shape[0] % 32 == 0 else 1
    own_kv, rows, own_routes, numer, *weights = prepare(
        matrix, queries[0], keys[0], values[0], routes[0].T, gate_numer, head_count, halves
    )

    weights = [swap(weights[m - 1], "head", m) for m in range(1, head_count)]

    kv_parts = spread(own_kv, "seq")
    gain = norm_gain.reshape(head_count, 1, share)

    gain, *attended = attend(
        sequence_lengths, rows, gain, own_routes, numer, kv_parts, count
    )
    if split:
        own_piece = attended[0]
        attended = swaps(attended, "seq")
        ahead = [swap(own_piece, "head", m) for m in range(1, head_count)] if count > 1 else []
        relayed = weights if halves == 2 else []
        mine, others, routing, *carried = pack(attended, tokens, relayed + ahead)
        carried, ahead = carried[: len(relayed)], carried[len(relayed) :]
    else:
        shares = attended[0].reshape(tokens, heads, count, part).transpose(2, 0, 1, 3)
        shares = shares.reshape(count * tokens, heads * part)
        mine = lax.all_to_all(shares, "seq", 0, 0, tiled=True)
        routing = jnp.concatenate(
            [own_routes, numer, jnp.zeros((5, tokens), jnp.int32)], axis=0
        )
        routing = lax.all_gather(routing, "seq", axis=1, tiled=True)
        carried = weights
    if halves == 2:
        weights = [[got, swap(again, "dat", 1)] for got, again in zip(weights, carried)]
    else:
        weights = [[got] for got in weights]
    own_weights = own_columns_of(matrix, share, mine)
    if split and count > 1:
        rows = [[mine]] + [
            [first, swap(others, "head", m + 1)] for m, first in enumerate(ahead)
        ]
    else:
        rows = [[mine]] + [[swap(mine, "head", m)] for m in range(1, head_count)]
    sums = project(rows, [[own_weights]] + weights, count if split else 1)
    chunk = min(256, expert_gate.shape[2])
    early = max(1, expert_gate.shape[0] * (expert_gate.shape[2] // chunk) * 12 // 16)
    *fetched, mixed = fetch(expert_gate, expert_up, sums[0], chunk, early)
    if split:
        received = swaps(sums, "seq")[1:]
        for part_sum in received[1:] + received[:1]:
            mixed = mixed + part_sum.astype(F32)
    else:
        mixed = lax.psum_scatter(mixed, "seq", scatter_dimension=0, tiled=True)

    stream = (residual_in[0].astype(F32) + mixed).astype(BF16)
    own_columns = spread(stream, "seq")
    columns = [own_columns] + [
        [swap(piece, "head", m) for piece in own_columns] for m in range(1, head_count)
    ]
    passes = [[0], list(range(1, head_count))] if head_count > 1 else [[0]]
    fetched_rows = fetch_rows(expert_gate, expert_up, stream, chunk, early, share)
    carried = [routing]
    for i, places in enumerate(passes):
        carried = run_experts(
            [columns[m] for m in places],
            tuple(places),
            gain,
            fetched,
            [] if i else fetched_rows,
            (expert_gate, expert_up),
            tokens,
            count,
            carried,
            i == len(passes) - 1,
        )
    hidden = carried[0]
    return (stream[None], hidden[:, None])


def solution(mesh):
    in_specs = (
        P(("grp", "dat"), "seq", "head"),
        P(("grp", "dat"), "seq", "head"),
        P(("grp", "dat"), "seq", "head"),
        P(("grp", "dat"), "seq", "head"),
        P("head", "seq", None),
        P(),
        P("head", None, "seq"),
        P("head", None, "seq"),
        P(("grp", "dat"), "seq", None),
        P(("grp", "dat"), "seq"),
        P(("grp", "dat")),
    )
    out_specs = (P(("grp", "dat"), "seq", "head"), P("head", ("grp", "dat"), None, "seq"))
    return jax.shard_map(local, mesh=mesh, in_specs=in_specs, out_specs=out_specs, check_vma=False)
```
